768 devices in a mesh: ctx: 64 (over x, y, core), head: 12 (over z).
Axes of the slice: x: 4, y: 8, z: 12, core: 2. Of those that a mesh axis runs over, the one named last changes fastest.
Arguments:
- hidden_in: bfloat16 [12288, 4096], P('ctx'), may hold values from -10 to 10
- query_soft: bfloat16 [12288, 3072], P('ctx', 'head'), may hold values from -6 to 6
- key_soft: bfloat16 [12288, 1536], P('ctx', 'head'), may hold values from -6 to 6
- value_soft: bfloat16 [12288, 1536], P('ctx', 'head'), may hold values from -6 to 6
- out_weight: bfloat16 [3072, 4096], P('head'), may hold values from -0.109375 to 0.109375
- query_weight: bfloat16 [4096, 3072], P(None, 'head'), may hold values from -0.09375 to 0.09375
- key_weight: bfloat16 [4096, 3072], P(None, 'head'), may hold values from -0.09375 to 0.09375
- value_weight: bfloat16 [4096, 3072], P(None, 'head'), may hold values from -0.09375 to 0.09375
Outputs:
- linear_out: bfloat16 [12288, 3072], P('ctx', 'head')
The draws below stay inside these ranges and needn't reach their ends.
All inputs are finite; a program needn't handle non-finite values.
Results may differ from the reference program's by a relative error of at most 0.025.
Values may be sent and summed in bfloat16 or wider, within the bound.
A program may use at most 64 MiB of HBM per device.

```python
import math
import jax
import jax.numpy as jnp
from jax import lax

D = 4096
HEAD_DIM = 128
HEAD_DEV = 2
TOK_DEV = 192
HEADS = 24
KV_HEADS = 12
TOKENS = 12288
N_CTX = 64


def row_scaled(key, row_count, column_count, low_scale, high_scale, clip_at):
    base_key = jax.random.fold_in(key, 1)
    scale_key = jax.random.fold_in(key, 2)
    base = jnp.clip(jax.random.normal(base_key, (row_count, column_count), jnp.float32), -clip_at, clip_at)
    row_scale = jnp.exp(jax.random.uniform(scale_key, (row_count, 1), jnp.float32, math.log(low_scale), math.log(high_scale)))
    return base * row_scale


def draw_hidden_in(key, part):
    rows_part = row_scaled(jax.random.fold_in(key, 11), TOKENS, D, 0.5, 2.0, 4.0)
    column_scale = jnp.exp(jax.random.uniform(jax.random.fold_in(key, 12), (1, D), jnp.float32, math.log(0.3), math.log(3.0)))
    return (0.4 * rows_part * column_scale).astype(jnp.bfloat16)


def drawn_pair(key):
    query_all = row_scaled(jax.random.fold_in(key, 21), TOKENS, HEADS * HEAD_DIM, 0.6, 2.4, 2.5)
    keys_all = row_scaled(jax.random.fold_in(key, 22), TOKENS, KV_HEADS * HEAD_DIM, 0.6, 2.4, 2.5)
    query_all = query_all.reshape(TOKENS, HEADS, HEAD_DIM)
    keys_all = keys_all.reshape(TOKENS, KV_HEADS, HEAD_DIM)
    return (query_all.reshape(TOKENS, HEADS * HEAD_DIM), keys_all.reshape(TOKENS, KV_HEADS * HEAD_DIM))


def draw_query_soft(key, part):
    return drawn_pair(key)[0].astype(jnp.bfloat16)


def draw_key_soft(key, part):
    return drawn_pair(key)[1].astype(jnp.bfloat16)


def levels(stream_key, extent, shards, smallest, largest):
    loudness, own = 1.0, jax.random.fold_in(stream_key, 6)
    for dim, blocks in shards:
        draws = jnp.exp(jax.random.uniform(jax.random.fold_in(own, dim), (blocks,), jnp.float32, smallest / len(shards), largest / len(shards)))
        loudness = loudness * jnp.repeat(draws, extent[dim] // blocks).reshape([-1 if axis == dim else 1 for axis in range(len(extent))])
    return loudness


def bell_draw(stream_key, dims, deviation, limit, pieces=(), kind=jnp.bfloat16):
    array = jax.random.normal(stream_key, dims, jnp.float32) * deviation
    if len(pieces) > 0:
        array = levels(stream_key, dims, pieces, -0.22, 0.18) * array
    return jnp.clip(array, min=-limit, max=limit).astype(kind)


def setup_inputs(seed: int = 0) -> dict:
    seeds = jax.random.split(jax.random.key(seed), 9)
    hidden_in = draw_hidden_in(jax.random.fold_in(seeds[8], 71), 0)
    query_soft = draw_query_soft(jax.random.fold_in(seeds[8], 71), 0)
    key_soft = draw_key_soft(jax.random.fold_in(seeds[8], 71), 0)
    value_soft = bell_draw(seeds[3], (TOKENS, KV_HEADS * HEAD_DIM), 1.0, 6.0, ((0, 64), (1, 12)))
    out_weight = bell_draw(seeds[4], (HEADS * HEAD_DIM, D), (HEADS * HEAD_DIM) ** -0.5, 0.109375, ((0, 12),))
    query_weight = bell_draw(seeds[5], (D, HEADS * HEAD_DIM), D ** -0.5, 0.09375, ((1, 12),))
    key_weight = bell_draw(seeds[6], (D, HEADS * HEAD_DIM), D ** -0.5, 0.09375, ((1, 12),))
    value_weight = bell_draw(seeds[7], (D, HEADS * HEAD_DIM), D ** -0.5, 0.09375, ((1, 12),))
    return dict(hidden_in=hidden_in, query_soft=query_soft, key_soft=key_soft, value_soft=value_soft, out_weight=out_weight, query_weight=query_weight, key_weight=key_weight, value_weight=value_weight)


def rms_rows(values):
    return values * lax.rsqrt(lax.optimization_barrier(jnp.mean(values * values, axis=-1, keepdims=True)) + 1e-06)

def rounded(values):
    return lax.optimization_barrier(values.astype(jnp.bfloat16)).astype(jnp.float32)

def reference(hidden_in, query_soft, key_soft, value_soft, out_weight, query_weight, key_weight, value_weight):
    float_type = jnp.float32
    keys_all = jnp.repeat(key_soft.reshape(TOKENS, KV_HEADS, HEAD_DIM), HEAD_DEV, axis=1).astype(float_type)
    values_all = jnp.repeat(value_soft.reshape(TOKENS, KV_HEADS, HEAD_DIM), HEAD_DEV, axis=1).astype(float_type)
    key_pos = jnp.arange(TOKENS, dtype=jnp.int32)
    query_blocks = query_soft.reshape(N_CTX, TOK_DEV, HEADS, HEAD_DIM)
    scale = 1.0 / math.sqrt(HEAD_DIM)

    def attend(block_args):
        block_query, block_index = block_args
        query_pos = block_index * TOK_DEV + jnp.arange(TOK_DEV, dtype=jnp.int32)
        scores = jnp.einsum('qhd,khd->hqk', block_query.astype(float_type), keys_all) * scale
        allowed = key_pos[None, None, :] <= query_pos[None, :, None]
        row_max = lax.optimization_barrier(jnp.max(jnp.where(allowed, scores, -1e+30), axis=-1, keepdims=True))
        exponent = jnp.where(allowed, jnp.exp(scores - row_max), 0.0)
        row_sum = lax.optimization_barrier(jnp.sum(exponent, axis=-1))
        weights = rounded(exponent)
        attended_block = jnp.einsum('hqk,khd->qhd', weights, values_all) / jnp.transpose(row_sum)[:, :, None]
        return attended_block.astype(jnp.bfloat16)
    attended = lax.map(attend, (query_blocks, jnp.arange(N_CTX, dtype=jnp.int32)))
    attended = attended.reshape(TOKENS, HEADS * HEAD_DIM)
    branch = jnp.dot(attended, out_weight, preferred_element_type=jnp.float32)
    normed = rms_rows(hidden_in.astype(float_type) + branch).astype(jnp.bfloat16)
    lin_query = rounded(jnp.dot(normed, query_weight, preferred_element_type=jnp.float32)).reshape(N_CTX, TOK_DEV, HEADS, HEAD_DIM)
    lin_key = rounded(jnp.dot(normed, key_weight, preferred_element_type=jnp.float32)).reshape(N_CTX, TOK_DEV, HEADS, HEAD_DIM)
    lin_value = rounded(jnp.dot(normed, value_weight, preferred_element_type=jnp.float32)).reshape(N_CTX, TOK_DEV, HEADS, HEAD_DIM)
    block_state = jnp.einsum('nthd,nthe->nhde', lin_key, lin_value)
    prefix = jnp.cumsum(block_state, axis=0)
    carried = jnp.concatenate([jnp.zeros_like(block_state[:1]), prefix[:-1]], axis=0)
    carried = rounded(carried)
    carried_part = jnp.einsum('nthd,nhde->nthe', lin_query, carried)
    local_scores = jnp.einsum('nthd,nshd->nhts', lin_query, lin_key)
    causal = jnp.arange(TOK_DEV, dtype=jnp.int32)[:, None] >= jnp.arange(TOK_DEV, dtype=jnp.int32)[None, :]
    local_scores = rounded(jnp.where(causal[None, None], local_scores, 0.0))
    mixed_rows = carried_part + jnp.einsum('nhts,nshe->nthe', local_scores, lin_value)
    return rms_rows(mixed_rows).astype(jnp.bfloat16).reshape(TOKENS, HEADS * HEAD_DIM)
```

```python
import math

import jax
import jax.numpy as jnp
from jax import lax
from jax.experimental import pallas as pl
from jax.experimental.pallas import tpu as pltpu
from jax.sharding import PartitionSpec as P

MESH = pl.DeviceIdType.MESH
HEAD = 128
TOK = 192
D = 4096
NX, NY, NZ = 4, 8, 12
SEG = 2 * NY
ROWS = TOK // NZ
PIECES = 4
WIDE = D // PIECES
QROWS = 2 * TOK
KROWS = 2 * TOK
C2 = math.log2(math.e) / math.sqrt(HEAD)
F32, BF16 = jnp.float32, jnp.bfloat16
NT = (((1,), (1,)), ((), ()))
TN = (((0,), (0,)), ((), ()))
DIST = (1, -1, 2, -2, 3, -3, 4)


def chain(direction, piece):
    return 6 if (direction == 0) == (piece < PIECES // 2) else 5


def kernel(
    hidden, query, key, value, w_out, w_q, w_k, w_v, out,
    hid, wo, wq, wk, wv,
    qb, kb, vb, vt, acc, stat, ob, mlb, po, pml, att,
    branch, rs_send, rs_recv, normed, proj,
    state, r1, tot, r2, ret, r3, keypad, mixed, before,
    load_sem,
    kv_ss, kv_rs, core_ss, core_rs, q_ss, q_rs, o_ss, o_rs,
    rs_ss, rs_rs, ag_ss, ag_rs, p1_ss, p1_rs, p2_ss, p2_rs, p3_ss, p3_rs,
):
    c = lax.axis_index("ctx")
    z = lax.axis_index("head")
    x, seg = c // SEG, c % SEG
    y, core = seg // 2, seg % 2

    def dev(xx, ss):
        return {"ctx": xx * SEG + ss, "head": z}

    def zdev(step):
        return {"ctx": c, "head": (z + step + NZ) % NZ}

    def ydev(step):
        return dev(x, ((y + step + NY) % NY) * 2 + core)

    partner = dev(x, y * 2 + (1 - core))

    def remote(src, dst, send, recv, to):
        return pltpu.make_async_remote_copy(
            src_ref=src, dst_ref=dst, send_sem=send, recv_sem=recv, device_id=to, device_id_type=MESH
        )

    loads = [
        pltpu.make_async_copy(w_out, wo, load_sem.at[0]),
        pltpu.make_async_copy(hidden.at[pl.ds(pl.multiple_of(z * ROWS, ROWS), ROWS)], hid, load_sem.at[1]),
        pltpu.make_async_copy(w_k, wk, load_sem.at[2]),
        pltpu.make_async_copy(w_v, wv, load_sem.at[3]),
        pltpu.make_async_copy(w_q, wq, load_sem.at[4]),
    ]
    for load in loads:
        load.start()

    barrier = pltpu.get_barrier_semaphore()
    for o in range(1, SEG):
        pl.semaphore_signal(barrier, inc=1, device_id=dev(x, (seg + o) % SEG), device_id_type=MESH)
    for o in range(1, NX):
        pl.semaphore_signal(barrier, inc=1, device_id=dev((x + o) % NX, seg), device_id_type=MESH)
    for o in (1, -1):
        pl.semaphore_signal(barrier, inc=1, device_id=zdev(o), device_id_type=MESH)

    own_rows = pl.ds(pl.multiple_of(core * TOK, TOK), TOK)
    other_rows = pl.ds(pl.multiple_of((1 - core) * TOK, TOK), TOK)
    qb[0, pl.ds(0, TOK), :] = query[:, pl.ds(0, HEAD)]
    qb[0, pl.ds(TOK, TOK), :] = query[:, pl.ds(HEAD, HEAD)]
    kb[y, own_rows, :] = key[...]
    vb[y, own_rows, :] = value[...]
    acc[...] = jnp.zeros_like(acc)
    stat[...] = jnp.zeros_like(stat)
    stat[:, 0, :] = jnp.full((NX, QROWS), -1e30, F32)
    pl.semaphore_wait(barrier, SEG - 1 + NX - 1 + 2)

    def kv_copy(i, which):
        d = DIST[i]
        buf = (kb, vb)[which]
        if abs(d) <= 2:
            source, step = y, d
        elif abs(d) == 3:
            sign = 1 if d > 0 else -1
            source, step = (y - 2 * sign + NY) % NY, sign
        else:
            sign = 1 if which == 0 else -1
            source, step = (y - 2 * sign + NY) % NY, 2 * sign
        ref = buf.at[source, own_rows]
        return remote(ref, ref, kv_ss.at[i, which], kv_rs.at[i, which], ydev(step))

    def kv_arrival(i, which):
        ref = (kb, vb)[which].at[(y - DIST[i] + NY) % NY, own_rows]
        return remote(ref, ref, kv_ss.at[i, which], kv_rs.at[i, which], partner)

    def core_copy(i, which):
        d = 0 if i == 0 else DIST[i - 1]
        ref = (kb, vb)[which].at[(y - d + NY) % NY, own_rows]
        return remote(ref, ref, core_ss.at[i, which], core_rs.at[i, which], partner)

    def core_arrival(i, which):
        d = 0 if i == 0 else DIST[i - 1]
        ref = (kb, vb)[which].at[(y - d + NY) % NY, other_rows]
        return remote(ref, ref, core_ss.at[i, which], core_rs.at[i, which], partner)

    def q_copy(o):
        return remote(qb.at[0], qb.at[o], q_ss.at[o], q_rs.at[o], dev((x - o + NX) % NX, seg))

    def o_copies(o):
        to = dev((x + o) % NX, seg)
        return (
            remote(ob.at[o], po.at[o], o_ss.at[o, 0], o_rs.at[o, 0], to),
            remote(mlb.at[o], pml.at[o], o_ss.at[o, 1], o_rs.at[o, 1], to),
        )

    for which in (0, 1):
        core_copy(0, which).start()
    for i in range(4):
        for which in (0, 1):
            kv_copy(i, which).start()
    for o in range(1, NX):
        @pl.when(x >= o)
        def _():
            q_copy(o).start()

    def unit(o, yk, masked):
        scores = lax.dot_general(kb[yk], qb[o], NT, preferred_element_type=F32)
        if masked:
            key_pos = lax.broadcasted_iota(jnp.int32, (KROWS, QROWS), 0)
            column = lax.broadcasted_iota(jnp.int32, (KROWS, QROWS), 1)
            query_pos = core * TOK + jnp.where(column >= TOK, column - TOK, column)
            scores = jnp.where(key_pos <= query_pos, scores, -1e30)
        old_max = stat[o, pl.ds(0, 1), :]
        new_max = jnp.maximum(old_max, jnp.max(scores, axis=0, keepdims=True))
        weights = jnp.exp2(scores * C2 - new_max * C2)
        factor = jnp.exp2((old_max - new_max) * C2)
        stat[o, pl.ds(0, 1), :] = new_max
        stat[o, pl.ds(1, 1), :] = stat[o, pl.ds(1, 1), :] * factor + jnp.sum(weights, axis=0, keepdims=True)
        acc[o] = acc[o] * factor + jnp.dot(vt[yk], weights.astype(BF16), preferred_element_type=F32)

    def turn_values(yk):
        vt[yk] = jnp.transpose(vb[yk].astype(F32)).astype(BF16)

    def later_units(yk):
        def step(o, carry):
            unit(o, yk, False)
            return carry

        lax.fori_loop(1, NX - x, step, 0)

    def group(first, stride, count):
        def step(e, carry):
            yk = (y + first + stride * e + 2 * NY) % NY
            turn_values(yk)

            @pl.when(yk < y)
            def _():
                unit(0, yk, False)

            later_units(yk)
            return carry

        lax.fori_loop(0, count, step, 0)

    for which in (0, 1):
        core_arrival(0, which).wait_recv()
    turn_values(y)
    unit(0, y, True)
    for o in range(1, NX):
        @pl.when(x + o < NX)
        def _():
            q_copy(o).wait_recv()
    later_units(y)

    def receive(indices, forwards):
        for i in indices:
            for which in (0, 1):
                kv_arrival(i, which).wait_recv()
                for j in forwards.get((i, which), ()):
                    kv_copy(j, which).start()
                core_copy(i + 1, which).start()
        for i in indices:
            for which in (0, 1):
                core_arrival(i + 1, which).wait_recv()

    receive((0, 1), {})
    group(-1, 2, 2)
    receive((2, 3), {(2, 0): (6, 4), (2, 1): (4,), (3, 0): (5,), (3, 1): (6, 5)})
    group(-2, 4, 2)
    receive((4, 5, 6), {})
    group(-3, -1, 3)

    for o in range(1, NX):
        @pl.when(x + o < NX)
        def _():
            ob[o] = acc[o].astype(BF16)
            mlb[o] = stat[o]
            for copy in o_copies(o):
                copy.start()

    loads[0].wait()

    for o in range(1, NX):
        @pl.when(x >= o)
        def _():
            for copy in o_copies(o):
                copy.wait_recv()
            old_max, part_max = stat[0, pl.ds(0, 1), :], pml[o, pl.ds(0, 1), :]
            new_max = jnp.maximum(old_max, part_max)
            factor = jnp.exp2((old_max - new_max) * C2)
            part_factor = jnp.exp2((part_max - new_max) * C2)
            stat[0, pl.ds(0, 1), :] = new_max
            stat[0, pl.ds(1, 1), :] = stat[0, pl.ds(1, 1), :] * factor + pml[o, pl.ds(1, 1), :] * part_factor
            acc[0] = acc[0] * factor + po[o].astype(F32) * part_factor

    attended = jnp.transpose(acc[0] / stat[0, pl.ds(1, 1), :])
    att[:, pl.ds(0, HEAD)] = attended[:TOK].astype(BF16)
    att[:, pl.ds(HEAD, HEAD)] = attended[TOK:].astype(BF16)

    def rs_copy(direction, step, piece):
        return remote(
            rs_send.at[direction, step, piece],
            rs_recv.at[direction, step, piece],
            rs_ss.at[direction, step, piece],
            rs_rs.at[direction, step, piece],
            zdev(-1 if direction == 0 else 1),
        )

    for step in range(6):
        for piece in range(PIECES):
            if step == 0:
                branch[:, :, pl.ds(piece * WIDE, WIDE)] = jnp.dot(
                    att[...], wo[:, pl.ds(piece * WIDE, WIDE)], preferred_element_type=F32
                ).reshape(NZ, ROWS, WIDE)
            for direction in (0, 1):
                length = chain(direction, piece)
                if step < length:
                    away = length - step
                    target = (z + (-away if direction == 0 else away) + NZ) % NZ
                    term = branch[target, :, pl.ds(piece * WIDE, WIDE)]
                    if step > 0:
                        rs_copy(direction, step - 1, piece).wait_recv()
                        term = term + rs_recv[direction, step - 1, piece].astype(F32)
                    rs_send[direction, step, piece] = term.astype(BF16)
                    rs_copy(direction, step, piece).start()

    loads[1].wait()
    square = jnp.zeros((ROWS, 1), F32)
    for piece in range(PIECES):
        columns = pl.ds(piece * WIDE, WIDE)
        total = branch[z, :, columns]
        for direction in (0, 1):
            last = chain(direction, piece) - 1
            rs_copy(direction, last, piece).wait_recv()
            total = total + rs_recv[direction, last, piece].astype(F32)
        total = total + hid[:, columns].astype(F32)
        branch[z, :, columns] = total
        square = square + jnp.sum(total * total, axis=1, keepdims=True)
    scale = lax.rsqrt(square * (1.0 / D) + 1e-6)

    def rows_of(step, direction):
        place = (z + (step if direction == 0 else -step) + NZ) % NZ
        return pl.ds(pl.multiple_of(place * ROWS, ROWS), ROWS)

    def ag_copy(direction, step, piece):
        ref = normed.at[rows_of(step, direction), pl.ds(piece * WIDE, WIDE)]
        return remote(
            ref, ref, ag_ss.at[direction, step, piece], ag_rs.at[direction, step, piece],
            zdev(-1 if direction == 0 else 1),
        )

    def ag_arrival(direction, step, piece):
        ref = normed.at[rows_of(step + 1, direction), pl.ds(piece * WIDE, WIDE)]
        return remote(
            ref, ref, ag_ss.at[direction, step, piece], ag_rs.at[direction, step, piece],
            zdev(-1 if direction == 0 else 1),
        )

    for piece in range(PIECES):
        columns = pl.ds(piece * WIDE, WIDE)
        normed[rows_of(0, 0), columns] = (branch[z, :, columns] * scale).astype(BF16)
        for direction in (0, 1):
            ag_copy(direction, 0, piece).start()
    for step in range(6):
        for piece in range(PIECES):
            for direction in (0, 1):
                length = chain(direction, piece)
                if step < length:
                    ag_arrival(direction, step, piece).wait_recv()
                    if step + 1 < length:
                        ag_copy(direction, step + 1, piece).start()

    for load in loads[2:]:
        load.wait()
    DEEP = 512

    def project(weight, slot):
        proj[slot] = jnp.zeros((TOK, 2 * HEAD), F32)

        def step(i, carry):
            deep = pl.ds(pl.multiple_of(i * DEEP, DEEP), DEEP)
            proj[slot] += jnp.dot(normed[:, deep], weight[deep, :], preferred_element_type=F32)
            return carry

        lax.fori_loop(0, D // DEEP, step, 0)

    project(wk, 1)
    project(wv, 2)

    keypad[...] = jnp.zeros_like(keypad)
    keypad[pl.ds(0, TOK), :] = proj[1].astype(BF16).astype(F32)
    for h in range(2):
        lanes = pl.ds(h * HEAD, HEAD)
        turned = jnp.transpose(keypad[:, lanes])[:, :TOK].astype(BF16)
        part = jnp.dot(turned, proj[2, :, lanes].astype(BF16), preferred_element_type=F32)
        state[pl.ds(h * (SEG // 2), SEG // 2)] = part.astype(BF16).reshape(SEG // 2, 16, HEAD)

    def p1_copy(o):
        return remote(state.at[(seg + o) % SEG], r1.at[seg], p1_ss.at[o], p1_rs.at[o], dev(x, (seg + o) % SEG))

    def p1_arrival(o):
        ref = r1.at[(seg - o + SEG) % SEG]
        return remote(ref, ref, p1_ss.at[o], p1_rs.at[o], partner)

    def p2_copy(o):
        return remote(tot, r2.at[o], p2_ss.at[o], p2_rs.at[o], dev((x + o) % NX, seg))

    def p3_copy(o):
        to = (seg + o) % SEG
        return remote(ret.at[to], r3.at[seg], p3_ss.at[o], p3_rs.at[o], dev(x, to))

    def p3_arrival(o):
        ref = r3.at[(seg - o + SEG) % SEG]
        return remote(ref, ref, p3_ss.at[o], p3_rs.at[o], partner)

    for o in range(1, SEG):
        p1_copy(o).start()
    r1[seg] = state[seg]
    project(wq, 0)
    for o in range(1, SEG):
        p1_arrival(o).wait_recv()
    run = jnp.zeros((16, HEAD), F32)
    for i in range(SEG):
        run = run + r1[i].astype(F32)
    tot[...] = run
    for o in range(1, NX):
        @pl.when(x + o < NX)
        def _():
            p2_copy(o).start()

    row = lax.broadcasted_iota(jnp.int32, (TOK, TOK), 0)
    column = lax.broadcasted_iota(jnp.int32, (TOK, TOK), 1)
    for h in range(2):
        lanes = pl.ds(h * HEAD, HEAD)
        near = lax.dot_general(
            proj[0, :, lanes].astype(BF16), proj[1, :, lanes].astype(BF16), NT, preferred_element_type=F32
        )
        near = jnp.where(row >= column, near, 0.0).astype(BF16)
        mixed[:, lanes] = jnp.dot(near, proj[2, :, lanes].astype(BF16), preferred_element_type=F32)

    before[...] = jnp.zeros_like(before)
    for o in range(1, NX):
        @pl.when(x >= o)
        def _():
            p2_copy(o).wait_recv()
            before[...] += r2[o]
    run = before[...]
    for i in range(SEG):
        ret[i] = run.astype(BF16)
        run = run + r1[i].astype(F32)
    for o in range(1, SEG):
        p3_copy(o).start()
    r3[seg] = ret[seg]
    for o in range(1, SEG):
        p3_arrival(o).wait_recv()

    for h in range(2):
        lanes = pl.ds(h * HEAD, HEAD)
        carried = r3[pl.ds(h * (SEG // 2), SEG // 2)].reshape(HEAD, HEAD)
        total = mixed[:, lanes] + jnp.dot(proj[0, :, lanes].astype(BF16), carried, preferred_element_type=F32)
        mean = jnp.mean(total * total, axis=1, keepdims=True)
        out[:, lanes] = (total * lax.rsqrt(mean + 1e-6)).astype(BF16)

    for which in (0, 1):
        for i in range(8):
            core_copy(i, which).wait_send()
        for i in range(7):
            kv_copy(i, which).wait_send()
    for o in range(1, NX):
        @pl.when(x >= o)
        def _():
            q_copy(o).wait_send()

        @pl.when(x + o < NX)
        def _():
            for copy in o_copies(o):
                copy.wait_send()
            p2_copy(o).wait_send()
    for direction in (0, 1):
        for piece in range(PIECES):
            for step in range(chain(direction, piece)):
                rs_copy(direction, step, piece).wait_send()
                ag_copy(direction, step, piece).wait_send()
    for o in range(1, SEG):
        p1_copy(o).wait_send()
        p3_copy(o).wait_send()


def body(*args):
    vmem = pl.BlockSpec(memory_space=pltpu.VMEM)
    anywhere = pl.BlockSpec(memory_space=pl.ANY)
    dma = pltpu.SemaphoreType.DMA
    scratch = [
        pltpu.VMEM((ROWS, D), BF16),
        pltpu.VMEM((2 * HEAD, D), BF16),
        pltpu.VMEM((D, 2 * HEAD), BF16),
        pltpu.VMEM((D, 2 * HEAD), BF16),
        pltpu.VMEM((D, 2 * HEAD), BF16),
        pltpu.VMEM((NX, QROWS, HEAD), BF16),
        pltpu.VMEM((NY, KROWS, HEAD), BF16),
        pltpu.VMEM((NY, KROWS, HEAD), BF16),
        pltpu.VMEM((NY, HEAD, KROWS), BF16),
        pltpu.VMEM((NX, HEAD, QROWS), F32),
        pltpu.VMEM((NX, 8, QROWS), F32),
        pltpu.VMEM((NX, HEAD, QROWS), BF16),
        pltpu.VMEM((NX, 8, QROWS), F32),
        pltpu.VMEM((NX, HEAD, QROWS), BF16),
        pltpu.VMEM((NX, 8, QROWS), F32),
        pltpu.VMEM((TOK, 2 * HEAD), BF16),
        pltpu.VMEM((NZ, ROWS, D), F32),
        pltpu.VMEM((2, 6, PIECES, ROWS, WIDE), BF16),
        pltpu.VMEM((2, 6, PIECES, ROWS, WIDE), BF16),
        pltpu.VMEM((TOK, D), BF16),
        pltpu.VMEM((3, TOK, 2 * HEAD), F32),
        pltpu.VMEM((SEG, 16, HEAD), BF16),
        pltpu.VMEM((SEG, 16, HEAD), BF16),
        pltpu.VMEM((16, HEAD), F32),
        pltpu.VMEM((NX, 16, HEAD), F32),
        pltpu.VMEM((SEG, 16, HEAD), BF16),
        pltpu.VMEM((SEG, 16, HEAD), BF16),
        pltpu.VMEM((2 * HEAD, 2 * HEAD), F32),
        pltpu.VMEM((TOK, 2 * HEAD), F32),
        pltpu.VMEM((16, HEAD), F32),
        dma((5,)),
        dma((7, 2)),
        dma((7, 2)),
        dma((8, 2)),
        dma((8, 2)),
        dma((NX,)),
        dma((NX,)),
        dma((NX, 2)),
        dma((NX, 2)),
        dma((2, 6, PIECES)),
        dma((2, 6, PIECES)),
        dma((2, 6, PIECES)),
        dma((2, 6, PIECES)),
        dma((SEG,)),
        dma((SEG,)),
        dma((NX,)),
        dma((NX,)),
        dma((SEG,)),
        dma((SEG,)),
    ]
    return pl.pallas_call(
        kernel,
        out_shape=jax.ShapeDtypeStruct((TOK, 2 * HEAD), BF16),
        in_specs=[anywhere, vmem, vmem, vmem, anywhere, anywhere, anywhere, anywhere],
        out_specs=vmem,
        scratch_shapes=scratch,
        compiler_params=pltpu.CompilerParams(
            collective_id=0, has_side_effects=True, vmem_limit_bytes=48 * 1024 * 1024
        ),
    )(*args)


def solution(mesh):
    return jax.shard_map(
        body,
        mesh=mesh,
        in_specs=(
            P("ctx", None),
            P("ctx", "head"),
            P("ctx", "head"),
            P("ctx", "head"),
            P("head", None),
            P(None, "head"),
            P(None, "head"),
            P(None, "head"),
        ),
        out_specs=P("ctx", "head"),
        check_vma=False,
    )
```

```python
import math

import jax
import jax.numpy as jnp
from jax import lax
from jax.experimental import pallas as pl
from jax.experimental.pallas import tpu as pltpu
from jax.sharding import PartitionSpec as P

MESH = pl.DeviceIdType.MESH
HEAD = 128
TOK = 192
D = 4096
NX, NY, NZ = 4, 8, 12
SEG = 2 * NY
ROWS = TOK // NZ
PIECES = 4
WIDE = D // PIECES
QROWS = 2 * TOK
KROWS = 2 * TOK
C2 = math.log2(math.e) / math.sqrt(HEAD)
F32, BF16 = jnp.float32, jnp.bfloat16
NT = (((1,), (1,)), ((), ()))
TN = (((0,), (0,)), ((), ()))
DIST = (1, -1, 2, -2, 3, -3, 4)
PAIRS = 4


def chain(direction, piece):
    return 6 if (direction == 0) == (piece < PIECES // 2) else 5


def kernel(
    hidden, query, key, value, w_out, w_q, w_k, w_v, out,
    hid, wo, wq, wk, wv,
    qin, qt, kb, vb, vt, acc, stat, ob, mlb, po, pml, att,
    branch, rs_send, rs_recv, normed, proj,
    state, r1, tot, r2, ret, r3, keypad, mixed, before,
    load_sem,
    kv_ss, kv_rs, core_ss, core_rs, q_ss, q_rs, o_ss, o_rs,
    rs_ss, rs_rs, ag_ss, ag_rs, p1_ss, p1_rs, p2_ss, p2_rs, p3_ss, p3_rs,
):
    c = lax.axis_index("ctx")
    z = lax.axis_index("head")
    x, seg = c // SEG, c % SEG
    y, core = seg // 2, seg % 2

    def dev(xx, ss):
        return {"ctx": xx * SEG + ss, "head": z}

    def zdev(step):
        return {"ctx": c, "head": (z + step + NZ) % NZ}

    def ydev(step):
        return dev(x, ((y + step + NY) % NY) * 2 + core)

    partner = dev(x, y * 2 + (1 - core))

    def remote(src, dst, send, recv, to):
        return pltpu.make_async_remote_copy(
            src_ref=src, dst_ref=dst, send_sem=send, recv_sem=recv, device_id=to, device_id_type=MESH
        )

    def half(buf, pair, place, mine=True):
        start = place * KROWS + (core if mine else 1 - core) * TOK
        return buf.at[pair, pl.ds(pl.multiple_of(start, TOK), TOK)]

    loads = [
        pltpu.make_async_copy(w_out, wo, load_sem.at[0]),
        pltpu.make_async_copy(hidden.at[pl.ds(pl.multiple_of(z * ROWS, ROWS), ROWS)], hid, load_sem.at[1]),
        pltpu.make_async_copy(w_k, wk, load_sem.at[2]),
        pltpu.make_async_copy(w_v, wv, load_sem.at[3]),
        pltpu.make_async_copy(w_q, wq, load_sem.at[4]),
    ]
    first_loads = [
        pltpu.make_async_copy(query, qin, load_sem.at[5]),
        pltpu.make_async_copy(key, half(kb, PAIRS - 1, 0), load_sem.at[6]),
        pltpu.make_async_copy(value, half(vb, PAIRS - 1, 0), load_sem.at[7]),
    ]
    for load in first_loads:
        load.start()

    barrier = pltpu.get_barrier_semaphore()
    for o in range(1, SEG):
        pl.semaphore_signal(barrier, inc=1, device_id=dev(x, (seg + o) % SEG), device_id_type=MESH)
    for o in range(1, NX):
        pl.semaphore_signal(barrier, inc=1, device_id=dev((x + o) % NX, seg), device_id_type=MESH)
    for o in (1, -1):
        pl.semaphore_signal(barrier, inc=1, device_id=zdev(o), device_id_type=MESH)

    for load in first_loads:
        load.wait()
    stacked = jnp.concatenate([qin[:, pl.ds(0, HEAD)], qin[:, pl.ds(HEAD, HEAD)]], axis=0)
    qt[0] = jnp.transpose(stacked.astype(F32)).astype(BF16)
    pl.semaphore_wait(barrier, SEG - 1 + NX - 1 + 2)

    def kv_copy(i, which):
        buf = (kb, vb)[which]
        if i < 4:
            source, step = half(buf, PAIRS - 1, 0), DIST[i]
        elif i < 6:
            source, step = half(buf, 1, i - 4), (1, -1)[i - 4]
        else:
            source, step = half(buf, 1, which), (2, -2)[which]
        target = half(buf, i // 2, i % 2 if i < 6 else 1)
        return remote(source, target, kv_ss.at[i, which], kv_rs.at[i, which], ydev(step))

    def kv_arrival(i, pair, place, which):
        ref = half((kb, vb)[which], pair, place)
        return remote(ref, ref, kv_ss.at[i, which], kv_rs.at[i, which], partner)

    def core_copy(i, pair, place, which):
        ref = half((kb, vb)[which], pair, place)
        return remote(ref, ref, core_ss.at[i, which], core_rs.at[i, which], partner)

    def core_arrival(i, pair, place, which):
        ref = half((kb, vb)[which], pair, place, False)
        return remote(ref, ref, core_ss.at[i, which], core_rs.at[i, which], partner)

    def q_copy(o):
        return remote(qt.at[0], qt.at[o], q_ss.at[o], q_rs.at[o], dev((x - o + NX) % NX, seg))

    def o_copies(o):
        to = dev((x + o) % NX, seg)
        return (
            remote(ob.at[o], po.at[o], o_ss.at[o, 0], o_rs.at[o, 0], to),
            remote(mlb.at[o], pml.at[o], o_ss.at[o, 1], o_rs.at[o, 1], to),
        )

    for i in (2, 3, 0, 1):
        for which in (0, 1):
            kv_copy(i, which).start()
    for which in (0, 1):
        core_copy(7, PAIRS - 1, 0, which).start()
    for o in range(1, NX):
        @pl.when(x >= o)
        def _():
            q_copy(o).start()
    for load in loads:
        load.start()

    def fold(o, scores, values):
        old_max = stat[o, pl.ds(0, 1), :]
        new_max = jnp.maximum(old_max, jnp.max(scores, axis=0, keepdims=True) * C2)
        weights = jnp.exp2(scores * C2 - new_max)
        factor = jnp.exp2(old_max - new_max)
        stat[o, pl.ds(0, 1), :] = new_max
        stat[o, pl.ds(1, 1), :] = stat[o, pl.ds(1, 1), :] * factor + jnp.sum(weights, axis=0, keepdims=True)
        acc[o] = acc[o] * factor + jnp.dot(values, weights.astype(BF16), preferred_element_type=F32)

    def turn_values(pair, place):
        rows = pl.ds(place * KROWS, KROWS)
        vt[pair, :, rows] = jnp.transpose(vb[pair, rows, :].astype(F32)).astype(BF16)

    acc[...] = jnp.zeros_like(acc)
    stat[...] = jnp.zeros_like(stat)
    stat[:, 0, :] = jnp.full((NX, QROWS), -1e30, F32)
    for which in (0, 1):
        core_arrival(7, PAIRS - 1, 0, which).wait_recv()
    turn_values(PAIRS - 1, 0)
    key_pos = lax.broadcasted_iota(jnp.int32, (KROWS, QROWS), 0)
    column = lax.broadcasted_iota(jnp.int32, (KROWS, QROWS), 1)
    query_pos = core * TOK + jnp.where(column >= TOK, column - TOK, column)
    own = jnp.dot(kb[PAIRS - 1, pl.ds(0, KROWS), :], qt[0], preferred_element_type=F32)
    fold(0, jnp.where(key_pos <= query_pos, own, -1e30), vt[PAIRS - 1, :, pl.ds(0, KROWS)])
    for o in range(1, NX):
        @pl.when(x + o < NX)
        def _():
            q_copy(o).wait_recv()

    def pair_step(pair, carry):
        @pl.when(pair < PAIRS - 1)
        def _():
            for place in (0, 1):
                for which in (0, 1):
                    i = 2 * pair + place
                    kv_arrival(i, pair, place, which).wait_recv()

                    @pl.when(pair == 1)
                    def _():
                        for j, w in {(0, 0): ((6, 0), (4, 0)), (0, 1): ((4, 1),), (1, 0): ((5, 0),), (1, 1): ((6, 1), (5, 1))}[place, which]:
                            kv_copy(j, w).start()

                    core_copy(i, pair, place, which).start()
            for place in (0, 1):
                for which in (0, 1):
                    core_arrival(2 * pair + place, pair, place, which).wait_recv()
            turn_values(pair, 0)

        @pl.when(pair == PAIRS - 1)
        def _():
            for which in (0, 1):
                kv_arrival(6, PAIRS - 1, 1, which).wait_recv()
                core_copy(6, PAIRS - 1, 1, which).start()
            for which in (0, 1):
                core_arrival(6, PAIRS - 1, 1, which).wait_recv()

        turn_values(pair, 1)

        last = pair == PAIRS - 1
        away = pair + 1
        seen_0 = jnp.logical_and(jnp.logical_not(last), y >= away)
        seen_1 = jnp.where(last, y >= away, y + away >= NY)
        bias_0 = jnp.where(seen_0, 0.0, -1e30).astype(F32)
        bias_1 = jnp.where(seen_1, 0.0, -1e30).astype(F32)
        for count in range(NX):
            @pl.when(x == NX - 1 - count)
            def _():
                found = [jnp.dot(kb[pair], qt[o], preferred_element_type=F32) for o in range(count + 1)]
                found[0] = jnp.concatenate([found[0][:KROWS] + bias_0, found[0][KROWS:] + bias_1], axis=0)
                for o in range(count + 1):
                    fold(o, found[o], vt[pair])
        return carry

    lax.fori_loop(0, PAIRS, pair_step, 0)

    for o in range(1, NX):
        @pl.when(x + o < NX)
        def _():
            ob[o] = acc[o].astype(BF16)
            mlb[o] = stat[o]
            for copy in o_copies(o):
                copy.start()

    loads[0].wait()

    for o in range(1, NX):
        @pl.when(x >= o)
        def _():
            for copy in o_copies(o):
                copy.wait_recv()
            old_max, part_max = stat[0, pl.ds(0, 1), :], pml[o, pl.ds(0, 1), :]
            new_max = jnp.maximum(old_max, part_max)
            factor = jnp.exp2(old_max - new_max)
            part_factor = jnp.exp2(part_max - new_max)
            stat[0, pl.ds(0, 1), :] = new_max
            stat[0, pl.ds(1, 1), :] = stat[0, pl.ds(1, 1), :] * factor + pml[o, pl.ds(1, 1), :] * part_factor
            acc[0] = acc[0] * factor + po[o].astype(F32) * part_factor

    attended = jnp.transpose(acc[0] / stat[0, pl.ds(1, 1), :])
    att[:, pl.ds(0, HEAD)] = attended[:TOK].astype(BF16)
    att[:, pl.ds(HEAD, HEAD)] = attended[TOK:].astype(BF16)

    def rs_copy(direction, step, piece):
        return remote(
            rs_send.at[direction, step, piece],
            rs_recv.at[direction, step, piece],
            rs_ss.at[direction, step, piece],
            rs_rs.at[direction, step, piece],
            zdev(-1 if direction == 0 else 1),
        )

    for step in range(6):
        for piece in range(PIECES):
            if step == 0:
                branch[:, :, pl.ds(piece * WIDE, WIDE)] = jnp.dot(
                    att[...], wo[:, pl.ds(piece * WIDE, WIDE)], preferred_element_type=F32
                ).reshape(NZ, ROWS, WIDE)
            for direction in (0, 1):
                length = chain(direction, piece)
                if step < length:
                    away = length - step
                    target = (z + (-away if direction == 0 else away) + NZ) % NZ
                    term = branch[target, :, pl.ds(piece * WIDE, WIDE)]
                    if step > 0:
                        rs_copy(direction, step - 1, piece).wait_recv()
                        term = term + rs_recv[direction, step - 1, piece].astype(F32)
                    rs_send[direction, step, piece] = term.astype(BF16)
                    rs_copy(direction, step, piece).start()

    def rows_of(step, direction):
        place = (z + (step if direction == 0 else -step) + NZ) % NZ
        return pl.ds(pl.multiple_of(place * ROWS, ROWS), ROWS)

    def ag_copy(direction, step, piece):
        ref = normed.at[rows_of(step, direction), pl.ds(piece * WIDE, WIDE)]
        return remote(
            ref, ref, ag_ss.at[direction, step, piece], ag_rs.at[direction, step, piece],
            zdev(-1 if direction == 0 else 1),
        )

    def ag_arrival(direction, step, piece):
        ref = normed.at[rows_of(step + 1, direction), pl.ds(piece * WIDE, WIDE)]
        return remote(
            ref, ref, ag_ss.at[direction, step, piece], ag_rs.at[direction, step, piece],
            zdev(-1 if direction == 0 else 1),
        )

    loads[1].wait()
    for piece in range(PIECES):
        columns = pl.ds(piece * WIDE, WIDE)
        total = branch[z, :, columns] + hid[:, columns].astype(F32)
        for direction in (0, 1):
            last = chain(direction, piece) - 1
            rs_copy(direction, last, piece).wait_recv()
            total = total + rs_recv[direction, last, piece].astype(F32)
        normed[rows_of(0, 0), columns] = total.astype(BF16)
        for direction in (0, 1):
            ag_copy(direction, 0, piece).start()

    def project(weight, slot, piece):
        columns = pl.ds(piece * WIDE, WIDE)
        proj[slot] += jnp.dot(normed[:, columns], weight[columns, :], preferred_element_type=F32)

    for load in loads[2:]:
        load.wait()
    proj[...] = jnp.zeros_like(proj)
    square = jnp.zeros((TOK, 1), F32)
    for step in range(6):
        for piece in range(PIECES):
            for direction in (0, 1):
                length = chain(direction, piece)
                if step < length:
                    ag_arrival(direction, step, piece).wait_recv()
                    if step + 1 < length:
                        ag_copy(direction, step + 1, piece).start()
            if step == 5:
                project(wk, 1, piece)
                project(wv, 2, piece)
                rows = normed[:, pl.ds(piece * WIDE, WIDE)].astype(F32)
                square = square + jnp.sum(rows * rows, axis=1, keepdims=True)
    scale = lax.rsqrt(square * (1.0 / D) + 1e-6)
    for slot in (1, 2):
        proj[slot] = proj[slot] * scale

    keypad[...] = jnp.zeros_like(keypad)
    keypad[pl.ds(0, TOK), :] = proj[1].astype(BF16).astype(F32)
    for h in range(2):
        lanes = pl.ds(h * HEAD, HEAD)
        turned = jnp.transpose(keypad[:, lanes])[:, :TOK].astype(BF16)
        part = jnp.dot(turned, proj[2, :, lanes].astype(BF16), preferred_element_type=F32)
        state[pl.ds(h * (SEG // 2), SEG // 2)] = part.astype(BF16).reshape(SEG // 2, 16, HEAD)

    def p1_copy(o):
        return remote(state.at[(seg + o) % SEG], r1.at[seg], p1_ss.at[o], p1_rs.at[o], dev(x, (seg + o) % SEG))

    def p1_arrival(o):
        ref = r1.at[(seg - o + SEG) % SEG]
        return remote(ref, ref, p1_ss.at[o], p1_rs.at[o], partner)

    def p2_copy(o):
        return remote(tot, r2.at[o], p2_ss.at[o], p2_rs.at[o], dev((x + o) % NX, seg))

    def p3_copy(o):
        to = (seg + o) % SEG
        return remote(ret.at[to], r3.at[seg], p3_ss.at[o], p3_rs.at[o], dev(x, to))

    def p3_arrival(o):
        ref = r3.at[(seg - o + SEG) % SEG]
        return remote(ref, ref, p3_ss.at[o], p3_rs.at[o], partner)

    for o in range(1, SEG):
        p1_copy(o).start()
    r1[seg] = state[seg]
    for piece in range(PIECES):
        project(wq, 0, piece)
    proj[0] = proj[0] * scale
    for o in range(1, SEG):
        p1_arrival(o).wait_recv()
    run = jnp.zeros((16, HEAD), F32)
    for i in range(SEG):
        run = run + r1[i].astype(F32)
    tot[...] = run
    for o in range(1, NX):
        @pl.when(x + o < NX)
        def _():
            p2_copy(o).start()

    row = lax.broadcasted_iota(jnp.int32, (TOK, TOK), 0)
    column = lax.broadcasted_iota(jnp.int32, (TOK, TOK), 1)
    for h in range(2):
        lanes = pl.ds(h * HEAD, HEAD)
        near = lax.dot_general(
            proj[0, :, lanes].astype(BF16), proj[1, :, lanes].astype(BF16), NT, preferred_element_type=F32
        )
        near = jnp.where(row >= column, near, 0.0).astype(BF16)
        mixed[:, lanes] = jnp.dot(near, proj[2, :, lanes].astype(BF16), preferred_element_type=F32)

    before[...] = jnp.zeros_like(before)
    for o in range(1, NX):
        @pl.when(x >= o)
        def _():
            p2_copy(o).wait_recv()
            before[...] += r2[o]
    run = before[...]
    for i in range(SEG):
        ret[i] = run.astype(BF16)
        run = run + r1[i].astype(F32)
    for o in range(1, SEG):
        p3_copy(o).start()
    r3[seg] = ret[seg]
    for o in range(1, SEG):
        p3_arrival(o).wait_recv()

    for h in range(2):
        lanes = pl.ds(h * HEAD, HEAD)
        carried = r3[pl.ds(h * (SEG // 2), SEG // 2)].reshape(HEAD, HEAD)
        total = mixed[:, lanes] + jnp.dot(proj[0, :, lanes].astype(BF16), carried, preferred_element_type=F32)
        mean = jnp.mean(total * total, axis=1, keepdims=True)
        out[:, lanes] = (total * lax.rsqrt(mean + 1e-6)).astype(BF16)

    for which in (0, 1):
        for i in range(8):
            core_copy(i, 0, 0, which).wait_send()
        for i in range(7):
            kv_copy(i, which).wait_send()
    for o in range(1, NX):
        @pl.when(x >= o)
        def _():
            q_copy(o).wait_send()

        @pl.when(x + o < NX)
        def _():
            for copy in o_copies(o):
                copy.wait_send()
            p2_copy(o).wait_send()
    for direction in (0, 1):
        for piece in range(PIECES):
            for step in range(chain(direction, piece)):
                rs_copy(direction, step, piece).wait_send()
                ag_copy(direction, step, piece).wait_send()
    for o in range(1, SEG):
        p1_copy(o).wait_send()
        p3_copy(o).wait_send()


def body(*args):
    vmem = pl.BlockSpec(memory_space=pltpu.VMEM)
    anywhere = pl.BlockSpec(memory_space=pl.ANY)
    dma = pltpu.SemaphoreType.DMA
    scratch = [
        pltpu.VMEM((ROWS, D), BF16),
        pltpu.VMEM((2 * HEAD, D), BF16),
        pltpu.VMEM((D, 2 * HEAD), BF16),
        pltpu.VMEM((D, 2 * HEAD), BF16),
        pltpu.VMEM((D, 2 * HEAD), BF16),
        pltpu.VMEM((TOK, 2 * HEAD), BF16),
        pltpu.VMEM((NX, HEAD, QROWS), BF16),
        pltpu.VMEM((PAIRS, 2 * KROWS, HEAD), BF16),
        pltpu.VMEM((PAIRS, 2 * KROWS, HEAD), BF16),
        pltpu.VMEM((PAIRS, HEAD, 2 * KROWS), BF16),
        pltpu.VMEM((NX, HEAD, QROWS), F32),
        pltpu.VMEM((NX, 8, QROWS), F32),
        pltpu.VMEM((NX, HEAD, QROWS), BF16),
        pltpu.VMEM((NX, 8, QROWS), F32),
        pltpu.VMEM((NX, HEAD, QROWS), BF16),
        pltpu.VMEM((NX, 8, QROWS), F32),
        pltpu.VMEM((TOK, 2 * HEAD), BF16),
        pltpu.VMEM((NZ, ROWS, D), F32),
        pltpu.VMEM((2, 6, PIECES, ROWS, WIDE), BF16),
        pltpu.VMEM((2, 6, PIECES, ROWS, WIDE), BF16),
        pltpu.VMEM((TOK, D), BF16),
        pltpu.VMEM((3, TOK, 2 * HEAD), F32),
        pltpu.VMEM((SEG, 16, HEAD), BF16),
        pltpu.VMEM((SEG, 16, HEAD), BF16),
        pltpu.VMEM((16, HEAD), F32),
        pltpu.VMEM((NX, 16, HEAD), F32),
        pltpu.VMEM((SEG, 16, HEAD), BF16),
        pltpu.VMEM((SEG, 16, HEAD), BF16),
        pltpu.VMEM((2 * HEAD, 2 * HEAD), F32),
        pltpu.VMEM((TOK, 2 * HEAD), F32),
        pltpu.VMEM((16, HEAD), F32),
        dma((8,)),
        dma((7, 2)),
        dma((7, 2)),
        dma((8, 2)),
        dma((8, 2)),
        dma((NX,)),
        dma((NX,)),
        dma((NX, 2)),
        dma((NX, 2)),
        dma((2, 6, PIECES)),
        dma((2, 6, PIECES)),
        dma((2, 6, PIECES)),
        dma((2, 6, PIECES)),
        dma((SEG,)),
        dma((SEG,)),
        dma((NX,)),
        dma((NX,)),
        dma((SEG,)),
        dma((SEG,)),
    ]
    return pl.pallas_call(
        kernel,
        out_shape=jax.ShapeDtypeStruct((TOK, 2 * HEAD), BF16),
        in_specs=[anywhere] * 8,
        out_specs=vmem,
        scratch_shapes=scratch,
        compiler_params=pltpu.CompilerParams(
            collective_id=0, has_side_effects=True, vmem_limit_bytes=60 * 1024 * 1024
        ),
    )(*args)


def solution(mesh):
    return jax.shard_map(
        body,
        mesh=mesh,
        in_specs=(
            P("ctx", None),
            P("ctx", "head"),
            P("ctx", "head"),
            P("ctx", "head"),
            P("head", None),
            P(None, "head"),
            P(None, "head"),
            P(None, "head"),
        ),
        out_specs=P("ctx", "head"),
        check_vma=False,
    )
```

```python
import math

import jax
import jax.numpy as jnp
from jax import lax
from jax.experimental import pallas as pl
from jax.experimental.pallas import tpu as pltpu
from jax.sharding import PartitionSpec as P

MESH = pl.DeviceIdType.MESH
HEAD = 128
TOK = 192
D = 4096
NX, NY, NZ = 4, 8, 12
SEG = 2 * NY
NPAIR = NZ // 2
ROWS = TOK // NZ
PIECES = 4
WIDE = D // PIECES
QROWS = 2 * TOK
KROWS = 2 * TOK
C2 = math.log2(math.e) / math.sqrt(HEAD)
F32, BF16 = jnp.float32, jnp.bfloat16
NT = (((1,), (1,)), ((), ()))
TN = (((0,), (0,)), ((), ()))
DIST = (1, -1, 2, -2, 3, -3, 4)
PAIRS = 4


def chain(direction, piece, far=6):
    return far if (direction == 0) == (piece < PIECES // 2) else far - 1


def kernel(
    hidden, query, key, value, w_out, w_q, w_k, w_v, out,
    hid, wo, wq, wk, wv,
    qin, qt, kb, vb, vt, acc, stat, ob, mlb, po, pml, att,
    branch, rs_send, rs_recv, normed, proj,
    att_in, state, r1, tot, r2, ret, r3, keypad, mixed, before,
    load_sem, w_ss, w_rs, a_ss, a_rs,
    kv_ss, kv_rs, core_ss, core_rs, q_ss, q_rs, o_ss, o_rs,
    rs_ss, rs_rs, ag_ss, ag_rs, p1_ss, p1_rs, p2_ss, p2_rs, p3_ss, p3_rs,
):
    c = lax.axis_index("ctx")
    z = lax.axis_index("head")
    x, seg = c // SEG, c % SEG
    y, core = seg // 2, seg % 2
    zpair, parity = z // 2, z % 2

    def dev(xx, ss):
        return {"ctx": xx * SEG + ss, "head": z}

    def zdev(step):
        return {"ctx": c, "head": (z + step + NZ) % NZ}

    def ydev(step):
        return dev(x, ((y + step + NY) % NY) * 2 + core)

    partner = dev(x, y * 2 + (1 - core))

    def remote(src, dst, send, recv, to):
        return pltpu.make_async_remote_copy(
            src_ref=src, dst_ref=dst, send_sem=send, recv_sem=recv, device_id=to, device_id_type=MESH
        )

    def half(buf, pair, place, mine=True):
        start = place * KROWS + (core if mine else 1 - core) * TOK
        return buf.at[pair, pl.ds(pl.multiple_of(start, TOK), TOK)]

    loads = [
        pltpu.make_async_copy(w_out, wo.at[pl.ds(0, 2 * HEAD)], load_sem.at[0]),
        pltpu.make_async_copy(hidden.at[pl.ds(pl.multiple_of(z * ROWS, ROWS), ROWS)], hid, load_sem.at[1]),
        pltpu.make_async_copy(w_k, wk, load_sem.at[2]),
        pltpu.make_async_copy(w_v, wv, load_sem.at[3]),
        pltpu.make_async_copy(w_q, wq, load_sem.at[4]),
    ]
    first_loads = [
        pltpu.make_async_copy(query, qin, load_sem.at[5]),
        pltpu.make_async_copy(key, half(kb, PAIRS - 1, 0), load_sem.at[6]),
        pltpu.make_async_copy(value, half(vb, PAIRS - 1, 0), load_sem.at[7]),
    ]
    for load in (*first_loads, loads[0]):
        load.start()

    barrier = pltpu.get_barrier_semaphore()
    for o in range(1, SEG):
        pl.semaphore_signal(barrier, inc=1, device_id=dev(x, (seg + o) % SEG), device_id_type=MESH)
    for o in range(1, NX):
        pl.semaphore_signal(barrier, inc=1, device_id=dev((x + o) % NX, seg), device_id_type=MESH)
    for o in (1, -1, 2, -2):
        pl.semaphore_signal(barrier, inc=1, device_id=zdev(o), device_id_type=MESH)

    for load in first_loads:
        load.wait()
    stacked = jnp.concatenate([qin[:, pl.ds(0, HEAD)], qin[:, pl.ds(HEAD, HEAD)]], axis=0)
    qt[0] = jnp.transpose(stacked.astype(F32)).astype(BF16)
    pl.semaphore_wait(barrier, SEG - 1 + NX - 1 + 4)

    def kv_copy(i, which):
        buf = (kb, vb)[which]
        if i < 4:
            source, step = half(buf, PAIRS - 1, 0), DIST[i]
        elif i < 6:
            source, step = half(buf, 1, i - 4), (1, -1)[i - 4]
        else:
            source, step = half(buf, 1, which), (2, -2)[which]
        target = half(buf, i // 2, i % 2 if i < 6 else 1)
        return remote(source, target, kv_ss.at[i, which], kv_rs.at[i, which], ydev(step))

    def kv_arrival(i, pair, place, which):
        ref = half((kb, vb)[which], pair, place)
        return remote(ref, ref, kv_ss.at[i, which], kv_rs.at[i, which], partner)

    def core_copy(i, pair, place, which):
        ref = half((kb, vb)[which], pair, place)
        return remote(ref, ref, core_ss.at[i, which], core_rs.at[i, which], partner)

    def core_arrival(i, pair, place, which):
        ref = half((kb, vb)[which], pair, place, False)
        return remote(ref, ref, core_ss.at[i, which], core_rs.at[i, which], partner)

    def q_copy(o):
        return remote(qt.at[0], qt.at[o], q_ss.at[o], q_rs.at[o], dev((x - o + NX) % NX, seg))

    def o_copies(o):
        to = dev((x + o) % NX, seg)
        return (
            remote(ob.at[o], po.at[o], o_ss.at[o, 0], o_rs.at[o, 0], to),
            remote(mlb.at[o], pml.at[o], o_ss.at[o, 1], o_rs.at[o, 1], to),
        )

    given = wo.at[pl.ds(pl.multiple_of(core * HEAD, HEAD), HEAD)]
    taken = wo.at[pl.ds(pl.multiple_of(2 * HEAD + core * HEAD, HEAD), HEAD)]
    twin = {"ctx": c, "head": zpair * 2 + 1 - parity}
    weight_copy = remote(given, taken, w_ss.at[0], w_rs.at[0], twin)
    weight_share = remote(taken, taken, w_ss.at[1], w_rs.at[1], partner)

    for i in (2, 3, 0, 1):
        for which in (0, 1):
            kv_copy(i, which).start()
    for which in (0, 1):
        core_copy(7, PAIRS - 1, 0, which).start()
    for o in range(1, NX):
        @pl.when(x >= o)
        def _():
            q_copy(o).start()
    loads[0].wait()
    weight_copy.start()
    for load in loads[1:]:
        load.start()

    def fold(o, scores, values):
        old_max = stat[o, pl.ds(0, 1), :]
        new_max = jnp.maximum(old_max, jnp.max(scores, axis=0, keepdims=True) * C2)
        weights = jnp.exp2(scores * C2 - new_max)
        factor = jnp.exp2(old_max - new_max)
        stat[o, pl.ds(0, 1), :] = new_max
        stat[o, pl.ds(1, 1), :] = stat[o, pl.ds(1, 1), :] * factor + jnp.sum(weights, axis=0, keepdims=True)
        acc[o] = acc[o] * factor + jnp.dot(values, weights.astype(BF16), preferred_element_type=F32)

    def turn_values(pair, place):
        rows = pl.ds(place * KROWS, KROWS)
        vt[pair, :, rows] = jnp.transpose(vb[pair, rows, :].astype(F32)).astype(BF16)

    acc[...] = jnp.zeros_like(acc)
    stat[...] = jnp.zeros_like(stat)
    stat[:, 0, :] = jnp.full((NX, QROWS), -1e30, F32)
    for which in (0, 1):
        core_arrival(7, PAIRS - 1, 0, which).wait_recv()
    turn_values(PAIRS - 1, 0)
    key_pos = lax.broadcasted_iota(jnp.int32, (KROWS, QROWS), 0)
    column = lax.broadcasted_iota(jnp.int32, (KROWS, QROWS), 1)
    query_pos = core * TOK + jnp.where(column >= TOK, column - TOK, column)
    own = jnp.dot(kb[PAIRS - 1, pl.ds(0, KROWS), :], qt[0], preferred_element_type=F32)
    fold(0, jnp.where(key_pos <= query_pos, own, -1e30), vt[PAIRS - 1, :, pl.ds(0, KROWS)])
    forwards = {(2, 0): ((6, 0), (4, 0)), (2, 1): ((4, 1),), (3, 0): ((5, 0),), (3, 1): ((6, 1), (5, 1))}

    def receive(i):
        pair, place = (i // 2, i % 2) if i < 6 else (PAIRS - 1, 1)
        for which in (0, 1):
            kv_arrival(i, pair, place, which).wait_recv()
            for j, w in forwards.get((i, which), ()):
                kv_copy(j, w).start()
            core_copy(i, pair, place, which).start()

    for i in (2, 3, 0, 1):
        receive(i)
    for o in range(1, NX):
        @pl.when(x + o < NX)
        def _():
            q_copy(o).wait_recv()

    def pair_step(pair, carry):
        @pl.when(pair == 2)
        def _():
            for i in (4, 5, 6):
                receive(i)

        @pl.when(pair < PAIRS - 1)
        def _():
            for place in (0, 1):
                for which in (0, 1):
                    core_arrival(2 * pair + place, pair, place, which).wait_recv()
            turn_values(pair, 0)

        @pl.when(pair == PAIRS - 1)
        def _():
            for which in (0, 1):
                core_arrival(6, PAIRS - 1, 1, which).wait_recv()

        turn_values(pair, 1)

        last = pair == PAIRS - 1
        away = pair + 1
        seen_0 = jnp.logical_and(jnp.logical_not(last), y >= away)
        seen_1 = jnp.where(last, y >= away, y + away >= NY)
        bias_0 = jnp.where(seen_0, 0.0, -1e30).astype(F32)
        bias_1 = jnp.where(seen_1, 0.0, -1e30).astype(F32)
        for count in range(NX):
            @pl.when(x == NX - 1 - count)
            def _():
                found = [jnp.dot(kb[pair], qt[o], preferred_element_type=F32) for o in range(count + 1)]
                found[0] = jnp.concatenate([found[0][:KROWS] + bias_0, found[0][KROWS:] + bias_1], axis=0)
                for o in range(count + 1):
                    fold(o, found[o], vt[pair])
        return carry

    lax.fori_loop(0, PAIRS, pair_step, 0)

    for o in range(1, NX):
        @pl.when(x + o < NX)
        def _():
            ob[o] = acc[o].astype(BF16)
            mlb[o] = stat[o]
            for copy in o_copies(o):
                copy.start()

    weight_copy.wait_recv()
    weight_share.start()

    for o in range(1, NX):
        @pl.when(x >= o)
        def _():
            for copy in o_copies(o):
                copy.wait_recv()
            old_max, part_max = stat[0, pl.ds(0, 1), :], pml[o, pl.ds(0, 1), :]
            new_max = jnp.maximum(old_max, part_max)
            factor = jnp.exp2(old_max - new_max)
            part_factor = jnp.exp2(part_max - new_max)
            stat[0, pl.ds(0, 1), :] = new_max
            stat[0, pl.ds(1, 1), :] = stat[0, pl.ds(1, 1), :] * factor + pml[o, pl.ds(1, 1), :] * part_factor
            acc[0] = acc[0] * factor + po[o].astype(F32) * part_factor

    attended = jnp.transpose(acc[0] / stat[0, pl.ds(1, 1), :])
    for chunk in range(NZ):
        for h in range(2):
            rows = attended[h * TOK + chunk * ROWS : h * TOK + (chunk + 1) * ROWS]
            att[chunk % 2, chunk // 2, :, pl.ds(h * HEAD, HEAD)] = rows.astype(BF16)

    att_copy = remote(att.at[1 - parity], att_in, a_ss.at[0], a_rs.at[0], twin)
    att_copy.start()
    branch[...] = jnp.zeros_like(branch)

    def project_out(rows, depth_start, piece):
        columns = pl.ds(piece * WIDE, WIDE)
        term = jnp.dot(
            rows.reshape(NPAIR * ROWS, 2 * HEAD), wo[pl.ds(depth_start, 2 * HEAD), columns], preferred_element_type=F32
        )
        branch[:, :, columns] += term.reshape(NPAIR, ROWS, WIDE)

    for piece in range(PIECES):
        project_out(att[parity], 0, piece)
    weight_share.wait_recv()
    att_copy.wait_recv()

    def rs_copy(direction, step, piece):
        return remote(
            rs_send.at[direction, step, piece],
            rs_recv.at[direction, step, piece],
            rs_ss.at[direction, step, piece],
            rs_rs.at[direction, step, piece],
            zdev(-2 if direction == 0 else 2),
        )

    for step in range(3):
        for piece in range(PIECES):
            if step == 0:
                project_out(att_in[...], 2 * HEAD, piece)
            for direction in (0, 1):
                length = chain(direction, piece, 3)
                if step < length:
                    away = length - step
                    target = (zpair + (-away if direction == 0 else away) + NPAIR) % NPAIR
                    term = branch[target, :, pl.ds(piece * WIDE, WIDE)]
                    if step > 0:
                        rs_copy(direction, step - 1, piece).wait_recv()
                        term = term + rs_recv[direction, step - 1, piece].astype(F32)
                    rs_send[direction, step, piece] = term.astype(BF16)
                    rs_copy(direction, step, piece).start()

    def rows_of(step, direction):
        place = (z + (step if direction == 0 else -step) + NZ) % NZ
        return pl.ds(pl.multiple_of(place * ROWS, ROWS), ROWS)

    def ag_copy(direction, step, piece):
        ref = normed.at[rows_of(step, direction), pl.ds(piece * WIDE, WIDE)]
        return remote(
            ref, ref, ag_ss.at[direction, step, piece], ag_rs.at[direction, step, piece],
            zdev(-1 if direction == 0 else 1),
        )

    def ag_arrival(direction, step, piece):
        ref = normed.at[rows_of(step + 1, direction), pl.ds(piece * WIDE, WIDE)]
        return remote(
            ref, ref, ag_ss.at[direction, step, piece], ag_rs.at[direction, step, piece],
            zdev(-1 if direction == 0 else 1),
        )

    loads[1].wait()
    for piece in range(PIECES):
        columns = pl.ds(piece * WIDE, WIDE)
        total = branch[zpair, :, columns] + hid[:, columns].astype(F32)
        for direction in (0, 1):
            last = chain(direction, piece, 3) - 1
            rs_copy(direction, last, piece).wait_recv()
            total = total + rs_recv[direction, last, piece].astype(F32)
        normed[rows_of(0, 0), columns] = total.astype(BF16)
        for direction in (0, 1):
            ag_copy(direction, 0, piece).start()

    def project(weight, slot, piece):
        columns = pl.ds(piece * WIDE, WIDE)
        proj[slot] += jnp.dot(normed[:, columns], weight[columns, :], preferred_element_type=F32)

    for load in loads[2:]:
        load.wait()
    proj[...] = jnp.zeros_like(proj)
    square = jnp.zeros((TOK, 1), F32)
    for step in range(6):
        for piece in range(PIECES):
            for direction in (0, 1):
                length = chain(direction, piece)
                if step < length:
                    ag_arrival(direction, step, piece).wait_recv()
                    if step + 1 < length:
                        ag_copy(direction, step + 1, piece).start()
            if step == 5:
                project(wk, 1, piece)
                project(wv, 2, piece)
                rows = normed[:, pl.ds(piece * WIDE, WIDE)].astype(F32)
                square = square + jnp.sum(rows * rows, axis=1, keepdims=True)
    scale = lax.rsqrt(square * (1.0 / D) + 1e-6)
    for slot in (1, 2):
        proj[slot] = proj[slot] * scale

    keypad[...] = jnp.zeros_like(keypad)
    keypad[pl.ds(0, TOK), :] = proj[1].astype(BF16).astype(F32)
    for h in range(2):
        lanes = pl.ds(h * HEAD, HEAD)
        turned = jnp.transpose(keypad[:, lanes])[:, :TOK].astype(BF16)
        part = jnp.dot(turned, proj[2, :, lanes].astype(BF16), preferred_element_type=F32)
        state[pl.ds(h * (SEG // 2), SEG // 2)] = part.astype(BF16).reshape(SEG // 2, 16, HEAD)

    def p1_copy(o):
        return remote(state.at[(seg + o) % SEG], r1.at[seg], p1_ss.at[o], p1_rs.at[o], dev(x, (seg + o) % SEG))

    def p1_arrival(o):
        ref = r1.at[(seg - o + SEG) % SEG]
        return remote(ref, ref, p1_ss.at[o], p1_rs.at[o], partner)

    def p2_copy(o):
        return remote(tot, r2.at[o], p2_ss.at[o], p2_rs.at[o], dev((x + o) % NX, seg))

    def p3_copy(o):
        to = (seg + o) % SEG
        return remote(ret.at[to], r3.at[seg], p3_ss.at[o], p3_rs.at[o], dev(x, to))

    def p3_arrival(o):
        ref = r3.at[(seg - o + SEG) % SEG]
        return remote(ref, ref, p3_ss.at[o], p3_rs.at[o], partner)

    for o in range(1, SEG):
        p1_copy(o).start()
    r1[seg] = state[seg]
    for piece in range(PIECES):
        project(wq, 0, piece)
    proj[0] = proj[0] * scale
    for o in range(1, SEG):
        p1_arrival(o).wait_recv()
    run = jnp.zeros((16, HEAD), F32)
    for i in range(SEG):
        run = run + r1[i].astype(F32)
    tot[...] = run
    for o in range(1, NX):
        @pl.when(x + o < NX)
        def _():
            p2_copy(o).start()

    row = lax.broadcasted_iota(jnp.int32, (TOK, TOK), 0)
    column = lax.broadcasted_iota(jnp.int32, (TOK, TOK), 1)
    for h in range(2):
        lanes = pl.ds(h * HEAD, HEAD)
        near = lax.dot_general(
            proj[0, :, lanes].astype(BF16), proj[1, :, lanes].astype(BF16), NT, preferred_element_type=F32
        )
        near = jnp.where(row >= column, near, 0.0).astype(BF16)
        mixed[:, lanes] = jnp.dot(near, proj[2, :, lanes].astype(BF16), preferred_element_type=F32)

    before[...] = jnp.zeros_like(before)
    for o in range(1, NX):
        @pl.when(x >= o)
        def _():
            p2_copy(o).wait_recv()
            before[...] += r2[o]
    run = before[...]
    for i in range(SEG):
        ret[i] = run.astype(BF16)
        run = run + r1[i].astype(F32)
    for o in range(1, SEG):
        p3_copy(o).start()
    r3[seg] = ret[seg]
    for o in range(1, SEG):
        p3_arrival(o).wait_recv()

    for h in range(2):
        lanes = pl.ds(h * HEAD, HEAD)
        carried = r3[pl.ds(h * (SEG // 2), SEG // 2)].reshape(HEAD, HEAD)
        total = mixed[:, lanes] + jnp.dot(proj[0, :, lanes].astype(BF16), carried, preferred_element_type=F32)
        mean = jnp.mean(total * total, axis=1, keepdims=True)
        out[:, lanes] = (total * lax.rsqrt(mean + 1e-6)).astype(BF16)

    for which in (0, 1):
        for i in range(8):
            core_copy(i, 0, 0, which).wait_send()
        for i in range(7):
            kv_copy(i, which).wait_send()
    for o in range(1, NX):
        @pl.when(x >= o)
        def _():
            q_copy(o).wait_send()

        @pl.when(x + o < NX)
        def _():
            for copy in o_copies(o):
                copy.wait_send()
            p2_copy(o).wait_send()
    for direction in (0, 1):
        for piece in range(PIECES):
            for step in range(chain(direction, piece, 3)):
                rs_copy(direction, step, piece).wait_send()
            for step in range(chain(direction, piece)):
                ag_copy(direction, step, piece).wait_send()
    weight_copy.wait_send()
    weight_share.wait_send()
    att_copy.wait_send()
    for o in range(1, SEG):
        p1_copy(o).wait_send()
        p3_copy(o).wait_send()


def body(*args):
    vmem = pl.BlockSpec(memory_space=pltpu.VMEM)
    anywhere = pl.BlockSpec(memory_space=pl.ANY)
    dma = pltpu.SemaphoreType.DMA
    scratch = [
        pltpu.VMEM((ROWS, D), BF16),
        pltpu.VMEM((4 * HEAD, D), BF16),
        pltpu.VMEM((D, 2 * HEAD), BF16),
        pltpu.VMEM((D, 2 * HEAD), BF16),
        pltpu.VMEM((D, 2 * HEAD), BF16),
        pltpu.VMEM((TOK, 2 * HEAD), BF16),
        pltpu.VMEM((NX, HEAD, QROWS), BF16),
        pltpu.VMEM((PAIRS, 2 * KROWS, HEAD), BF16),
        pltpu.VMEM((PAIRS, 2 * KROWS, HEAD), BF16),
        pltpu.VMEM((PAIRS, HEAD, 2 * KROWS), BF16),
        pltpu.VMEM((NX, HEAD, QROWS), F32),
        pltpu.VMEM((NX, 8, QROWS), F32),
        pltpu.VMEM((NX, HEAD, QROWS), BF16),
        pltpu.VMEM((NX, 8, QROWS), F32),
        pltpu.VMEM((NX, HEAD, QROWS), BF16),
        pltpu.VMEM((NX, 8, QROWS), F32),
        pltpu.VMEM((2, NPAIR, ROWS, 2 * HEAD), BF16),
        pltpu.VMEM((NPAIR, ROWS, D), F32),
        pltpu.VMEM((2, 3, PIECES, ROWS, WIDE), BF16),
        pltpu.VMEM((2, 3, PIECES, ROWS, WIDE), BF16),
        pltpu.VMEM((TOK, D), BF16),
        pltpu.VMEM((3, TOK, 2 * HEAD), F32),
        pltpu.VMEM((NPAIR, ROWS, 2 * HEAD), BF16),
        pltpu.VMEM((SEG, 16, HEAD), BF16),
        pltpu.VMEM((SEG, 16, HEAD), BF16),
        pltpu.VMEM((16, HEAD), F32),
        pltpu.VMEM((NX, 16, HEAD), F32),
        pltpu.VMEM((SEG, 16, HEAD), BF16),
        pltpu.VMEM((SEG, 16, HEAD), BF16),
        pltpu.VMEM((2 * HEAD, 2 * HEAD), F32),
        pltpu.VMEM((TOK, 2 * HEAD), F32),
        pltpu.VMEM((16, HEAD), F32),
        dma((8,)),
        dma((2,)),
        dma((2,)),
        dma((1,)),
        dma((1,)),
        dma((7, 2)),
        dma((7, 2)),
        dma((8, 2)),
        dma((8, 2)),
        dma((NX,)),
        dma((NX,)),
        dma((NX, 2)),
        dma((NX, 2)),
        dma((2, 3, PIECES)),
        dma((2, 3, PIECES)),
        dma((2, 6, PIECES)),
        dma((2, 6, PIECES)),
        dma((SEG,)),
        dma((SEG,)),
        dma((NX,)),
        dma((NX,)),
        dma((SEG,)),
        dma((SEG,)),
    ]
    return pl.pallas_call(
        kernel,
        out_shape=jax.ShapeDtypeStruct((TOK, 2 * HEAD), BF16),
        in_specs=[anywhere] * 8,
        out_specs=vmem,
        scratch_shapes=scratch,
        compiler_params=pltpu.CompilerParams(
            collective_id=0, has_side_effects=True, vmem_limit_bytes=60 * 1024 * 1024
        ),
    )(*args)


def solution(mesh):
    return jax.shard_map(
        body,
        mesh=mesh,
        in_specs=(
            P("ctx", None),
            P("ctx", "head"),
            P("ctx", "head"),
            P("ctx", "head"),
            P("head", None),
            P(None, "head"),
            P(None, "head"),
            P(None, "head"),
        ),
        out_specs=P("ctx", "head"),
        check_vma=False,
    )
```

```python
import math

import jax
import jax.numpy as jnp
from jax import lax
from jax.experimental import pallas as pl
from jax.experimental.pallas import tpu as pltpu
from jax.sharding import PartitionSpec as P

MESH = pl.DeviceIdType.MESH
HEAD = 128
TOK = 192
D = 4096
NX, NY, NZ = 4, 8, 12
SEG = 2 * NY
NPAIR = NZ // 2
ROWS = TOK // NZ
PIECES = 8
WIDE = D // PIECES
QROWS = 2 * TOK
KROWS = 2 * TOK
C2 = math.log2(math.e) / math.sqrt(HEAD)
F32, BF16 = jnp.float32, jnp.bfloat16
NT = (((1,), (1,)), ((), ()))
TN = (((0,), (0,)), ((), ()))
DIST = (1, -1, 2, -2, 3, -3, 4)
PAIRS = 4
PARENT = {1: 0, 2: 1, 3: 2, 4: 2, 5: 4, 6: 4}
FAR_FIRST = sorted(range(1, SEG), key=lambda o: -min(o, SEG - o))


def chain(direction, piece, far=6):
    return far if (direction == 0) == (piece < PIECES // 2) else far - 1


def kernel(
    hidden, query, key, value, w_out, w_q, w_k, w_v, out,
    hid, wo, wq, wk, wv,
    qin, qt, kb, vb, vt, acc, stat, ob, mlb, po, pml, att,
    branch, rs_send, rs_recv, normed, proj,
    att_in, state, r1, tot, r2, ret, r3, keypad, mixed, before,
    load_sem, w_ss, w_rs, a_ss, a_rs,
    kv_ss, kv_rs, core_ss, core_rs, q_ss, q_rs, o_ss, o_rs,
    rs_ss, rs_rs, ag_ss, ag_rs, p1_ss, p1_rs, p2_ss, p2_rs, p3_ss, p3_rs,
):
    c = lax.axis_index("ctx")
    z = lax.axis_index("head")
    x, seg = c // SEG, c % SEG
    y, core = seg // 2, seg % 2
    zpair, parity = z // 2, z % 2

    def dev(xx, ss):
        return {"ctx": xx * SEG + ss, "head": z}

    def zdev(step):
        return {"ctx": c, "head": (z + step + NZ) % NZ}

    def ydev(step):
        return dev(x, ((y + step + NY) % NY) * 2 + core)

    partner = dev(x, y * 2 + (1 - core))

    def remote(src, dst, send, recv, to):
        return pltpu.make_async_remote_copy(
            src_ref=src, dst_ref=dst, send_sem=send, recv_sem=recv, device_id=to, device_id_type=MESH
        )

    def half(buf, pair, place, mine=True):
        start = place * KROWS + (core if mine else 1 - core) * TOK
        return buf.at[pair, pl.ds(pl.multiple_of(start, TOK), TOK)]

    loads = [
        pltpu.make_async_copy(w_out, wo.at[pl.ds(0, 2 * HEAD)], load_sem.at[0]),
        pltpu.make_async_copy(hidden.at[pl.ds(pl.multiple_of(z * ROWS, ROWS), ROWS)], hid, load_sem.at[1]),
        pltpu.make_async_copy(w_k, wk, load_sem.at[2]),
        pltpu.make_async_copy(w_v, wv, load_sem.at[3]),
        pltpu.make_async_copy(w_q, wq, load_sem.at[4]),
    ]
    first_loads = [
        pltpu.make_async_copy(query, qin, load_sem.at[5]),
        pltpu.make_async_copy(key, half(kb, PAIRS - 1, 0), load_sem.at[6]),
        pltpu.make_async_copy(value, half(vb, PAIRS - 1, 0), load_sem.at[7]),
    ]
    for load in (*first_loads, loads[0]):
        load.start()

    barrier = pltpu.get_barrier_semaphore()
    for o in range(1, SEG):
        pl.semaphore_signal(barrier, inc=1, device_id=dev(x, (seg + o) % SEG), device_id_type=MESH)
    for o in range(1, NX):
        pl.semaphore_signal(barrier, inc=1, device_id=dev((x + o) % NX, seg), device_id_type=MESH)
    for o in (1, -1, 2, -2):
        pl.semaphore_signal(barrier, inc=1, device_id=zdev(o), device_id_type=MESH)

    for load in first_loads:
        load.wait()
    stacked = jnp.concatenate([qin[:, pl.ds(0, HEAD)], qin[:, pl.ds(HEAD, HEAD)]], axis=0)
    qt[0] = jnp.transpose(stacked.astype(F32)).astype(BF16)
    pl.semaphore_wait(barrier, SEG - 1 + NX - 1 + 4)

    def kv_copy(i, which):
        buf = (kb, vb)[which]
        if i < 4:
            source, step = half(buf, PAIRS - 1, 0), DIST[i]
        elif i < 6:
            source, step = half(buf, 1, i - 4), (1, -1)[i - 4]
        else:
            source, step = half(buf, 1, which), (2, -2)[which]
        target = half(buf, i // 2, i % 2 if i < 6 else 1)
        return remote(source, target, kv_ss.at[i, which], kv_rs.at[i, which], ydev(step))

    def kv_arrival(i, pair, place, which):
        ref = half((kb, vb)[which], pair, place)
        return remote(ref, ref, kv_ss.at[i, which], kv_rs.at[i, which], partner)

    def core_copy(i, pair, place, which):
        ref = half((kb, vb)[which], pair, place)
        return remote(ref, ref, core_ss.at[i, which], core_rs.at[i, which], partner)

    def core_arrival(i, pair, place, which):
        ref = half((kb, vb)[which], pair, place, False)
        return remote(ref, ref, core_ss.at[i, which], core_rs.at[i, which], partner)

    def q_copy(o):
        return remote(qt.at[0], qt.at[o], q_ss.at[o], q_rs.at[o], dev((x - o + NX) % NX, seg))

    def o_copies(o):
        to = dev((x + o) % NX, seg)
        return (
            remote(ob.at[o], po.at[o], o_ss.at[o, 0], o_rs.at[o, 0], to),
            remote(mlb.at[o], pml.at[o], o_ss.at[o, 1], o_rs.at[o, 1], to),
        )

    given = wo.at[pl.ds(pl.multiple_of(core * HEAD, HEAD), HEAD)]
    taken = wo.at[pl.ds(pl.multiple_of(2 * HEAD + core * HEAD, HEAD), HEAD)]
    twin = {"ctx": c, "head": zpair * 2 + 1 - parity}
    weight_copy = remote(given, taken, w_ss.at[0], w_rs.at[0], twin)
    weight_share = remote(taken, taken, w_ss.at[1], w_rs.at[1], partner)

    for i in (2, 3, 0, 1):
        for which in (0, 1):
            kv_copy(i, which).start()
    for which in (0, 1):
        core_copy(7, PAIRS - 1, 0, which).start()
    for o in range(1, NX):
        @pl.when(x >= o)
        def _():
            q_copy(o).start()
    loads[0].wait()
    weight_copy.start()
    for load in loads[1:]:
        load.start()

    def fold(o, scores, values):
        old_max = stat[o, pl.ds(0, 1), :]
        new_max = jnp.maximum(old_max, jnp.max(scores, axis=0, keepdims=True) * C2)
        weights = jnp.exp2(scores * C2 - new_max)
        factor = jnp.exp2(old_max - new_max)
        stat[o, pl.ds(0, 1), :] = new_max
        stat[o, pl.ds(1, 1), :] = stat[o, pl.ds(1, 1), :] * factor + jnp.sum(weights, axis=0, keepdims=True)
        acc[o] = acc[o] * factor + jnp.dot(values, weights.astype(BF16), preferred_element_type=F32)

    def turn_values(pair, place):
        rows = pl.ds(place * KROWS, KROWS)
        vt[pair, :, rows] = jnp.transpose(vb[pair, rows, :].astype(F32)).astype(BF16)

    acc[...] = jnp.zeros_like(acc)
    stat[...] = jnp.zeros_like(stat)
    stat[:, 0, :] = jnp.full((NX, QROWS), -1e30, F32)
    for which in (0, 1):
        core_arrival(7, PAIRS - 1, 0, which).wait_recv()
    turn_values(PAIRS - 1, 0)
    key_pos = lax.broadcasted_iota(jnp.int32, (KROWS, QROWS), 0)
    column = lax.broadcasted_iota(jnp.int32, (KROWS, QROWS), 1)
    query_pos = core * TOK + jnp.where(column >= TOK, column - TOK, column)
    own = jnp.dot(kb[PAIRS - 1, pl.ds(0, KROWS), :], qt[0], preferred_element_type=F32)
    fold(0, jnp.where(key_pos <= query_pos, own, -1e30), vt[PAIRS - 1, :, pl.ds(0, KROWS)])
    forwards = {(2, 0): ((6, 0), (4, 0)), (2, 1): ((4, 1),), (3, 0): ((5, 0),), (3, 1): ((6, 1), (5, 1))}

    def receive(i):
        pair, place = (i // 2, i % 2) if i < 6 else (PAIRS - 1, 1)
        for which in (0, 1):
            kv_arrival(i, pair, place, which).wait_recv()
            for j, w in forwards.get((i, which), ()):
                kv_copy(j, w).start()
            core_copy(i, pair, place, which).start()

    for i in (2, 3, 0, 1):
        receive(i)
    for o in range(1, NX):
        @pl.when(x + o < NX)
        def _():
            q_copy(o).wait_recv()

    def pair_step(pair, carry):
        @pl.when(pair == 2)
        def _():
            for i in (4, 5, 6):
                receive(i)

        @pl.when(pair < PAIRS - 1)
        def _():
            for place in (0, 1):
                for which in (0, 1):
                    core_arrival(2 * pair + place, pair, place, which).wait_recv()
            turn_values(pair, 0)

        @pl.when(pair == PAIRS - 1)
        def _():
            for which in (0, 1):
                core_arrival(6, PAIRS - 1, 1, which).wait_recv()

        turn_values(pair, 1)

        last = pair == PAIRS - 1
        away = pair + 1
        seen_0 = jnp.logical_and(jnp.logical_not(last), y >= away)
        seen_1 = jnp.where(last, y >= away, y + away >= NY)
        bias_0 = jnp.where(seen_0, 0.0, -1e30).astype(F32)
        bias_1 = jnp.where(seen_1, 0.0, -1e30).astype(F32)
        for count in range(NX):
            @pl.when(x == NX - 1 - count)
            def _():
                found = [jnp.dot(kb[pair], qt[o], preferred_element_type=F32) for o in range(count + 1)]
                found[0] = jnp.concatenate([found[0][:KROWS] + bias_0, found[0][KROWS:] + bias_1], axis=0)
                for o in range(count + 1):
                    fold(o, found[o], vt[pair])
        return carry

    lax.fori_loop(0, PAIRS, pair_step, 0)

    for o in range(1, NX):
        @pl.when(x + o < NX)
        def _():
            ob[o] = acc[o].astype(BF16)
            mlb[o] = stat[o]
            for copy in o_copies(o):
                copy.start()

    weight_copy.wait_recv()
    weight_share.start()

    for o in range(1, NX):
        @pl.when(x >= o)
        def _():
            for copy in o_copies(o):
                copy.wait_recv()
            old_max, part_max = stat[0, pl.ds(0, 1), :], pml[o, pl.ds(0, 1), :]
            new_max = jnp.maximum(old_max, part_max)
            factor = jnp.exp2(old_max - new_max)
            part_factor = jnp.exp2(part_max - new_max)
            stat[0, pl.ds(0, 1), :] = new_max
            stat[0, pl.ds(1, 1), :] = stat[0, pl.ds(1, 1), :] * factor + pml[o, pl.ds(1, 1), :] * part_factor
            acc[0] = acc[0] * factor + po[o].astype(F32) * part_factor

    attended = jnp.transpose(acc[0] / stat[0, pl.ds(1, 1), :])
    for chunk in range(NZ):
        for h in range(2):
            rows = attended[h * TOK + chunk * ROWS : h * TOK + (chunk + 1) * ROWS]
            att[chunk % 2, chunk // 2, :, pl.ds(h * HEAD, HEAD)] = rows.astype(BF16)

    att_copy = remote(att.at[1 - parity], att_in, a_ss.at[0], a_rs.at[0], twin)
    att_copy.start()

    def project_out(rows, depth_start, piece):
        columns = pl.ds(piece * WIDE, WIDE)
        term = jnp.dot(
            rows.reshape(NPAIR * ROWS, 2 * HEAD), wo[pl.ds(depth_start, 2 * HEAD), columns], preferred_element_type=F32
        )
        return columns, term.reshape(NPAIR, ROWS, WIDE)

    for piece in range(PIECES):
        columns, term = project_out(att[parity], 0, piece)
        branch[:, :, columns] = term
    weight_share.wait_recv()
    att_copy.wait_recv()

    def rs_copy(direction, step, piece):
        return remote(
            rs_send.at[direction, step, piece],
            rs_recv.at[direction, step, piece],
            rs_ss.at[direction, step, piece],
            rs_rs.at[direction, step, piece],
            zdev(-2 if direction == 0 else 2),
        )

    for step in range(3):
        for piece in range(PIECES):
            if step == 0:
                columns, term = project_out(att_in[...], 2 * HEAD, piece)
                branch[:, :, columns] += term
            for direction in (0, 1):
                length = chain(direction, piece, 3)
                if step < length:
                    away = length - step
                    target = (zpair + (-away if direction == 0 else away) + NPAIR) % NPAIR
                    term = branch[target, :, pl.ds(piece * WIDE, WIDE)]
                    if step > 0:
                        rs_copy(direction, step - 1, piece).wait_recv()
                        term = term + rs_recv[direction, step - 1, piece].astype(F32)
                    rs_send[direction, step, piece] = term.astype(BF16)
                    rs_copy(direction, step, piece).start()

    def rows_of(direction, distance, piece):
        place = (z + (distance if direction == 0 else -distance) + NZ) % NZ
        rows = pl.ds(pl.multiple_of(place * ROWS, ROWS), ROWS)
        return normed.at[rows, pl.ds(piece * WIDE, WIDE)]

    def ag_remote(ref, direction, distance, piece, step):
        return remote(
            ref, ref, ag_ss.at[direction, distance - 1, piece], ag_rs.at[direction, distance - 1, piece],
            zdev(-step if direction == 0 else step),
        )

    def ag_copy(direction, distance, piece):
        parent = PARENT[distance]
        return ag_remote(rows_of(direction, parent, piece), direction, distance, piece, distance - parent)

    def ag_arrival(direction, distance, piece):
        return ag_remote(rows_of(direction, distance, piece), direction, distance, piece, 1)

    def pass_on(direction, distance, piece):
        for farther in (6, 5, 4, 3, 2, 1):
            if PARENT[farther] == distance and farther <= chain(direction, piece):
                ag_copy(direction, farther, piece).start()

    loads[1].wait()
    for piece in range(PIECES):
        columns = pl.ds(piece * WIDE, WIDE)
        total = branch[zpair, :, columns] + hid[:, columns].astype(F32)
        for direction in (0, 1):
            last = chain(direction, piece, 3) - 1
            rs_copy(direction, last, piece).wait_recv()
            total = total + rs_recv[direction, last, piece].astype(F32)
        normed[pl.ds(pl.multiple_of(z * ROWS, ROWS), ROWS), columns] = total.astype(BF16)
        for direction in (0, 1):
            pass_on(direction, 0, piece)

    def project(weight, slot, piece):
        columns = pl.ds(piece * WIDE, WIDE)
        proj[slot] += jnp.dot(normed[:, columns], weight[columns, :], preferred_element_type=F32)

    for load in loads[2:]:
        load.wait()
    proj[...] = jnp.zeros_like(proj)
    square = jnp.zeros((TOK, 1), F32)
    for distance in (1, 2, 4, 3, 6, 5):
        for piece in range(PIECES):
            for direction in (0, 1):
                if distance <= chain(direction, piece):
                    ag_arrival(direction, distance, piece).wait_recv()
                    pass_on(direction, distance, piece)
            if distance == 5:
                project(wk, 1, piece)
                project(wv, 2, piece)
                rows = normed[:, pl.ds(piece * WIDE, WIDE)].astype(F32)
                square = square + jnp.sum(rows * rows, axis=1, keepdims=True)
    scale = lax.rsqrt(square * (1.0 / D) + 1e-6)
    for slot in (1, 2):
        proj[slot] = proj[slot] * scale

    keypad[...] = jnp.zeros_like(keypad)
    keypad[pl.ds(0, TOK), :] = proj[1].astype(BF16).astype(F32)
    for h in range(2):
        lanes = pl.ds(h * HEAD, HEAD)
        turned = jnp.transpose(keypad[:, lanes])[:, :TOK].astype(BF16)
        part = jnp.dot(turned, proj[2, :, lanes].astype(BF16), preferred_element_type=F32)
        state[pl.ds(h * (SEG // 2), SEG // 2)] = part.astype(BF16).reshape(SEG // 2, 16, HEAD)

    def p1_copy(o):
        return remote(state.at[(seg + o) % SEG], r1.at[seg], p1_ss.at[o], p1_rs.at[o], dev(x, (seg + o) % SEG))

    def p1_arrival(o):
        ref = r1.at[(seg - o + SEG) % SEG]
        return remote(ref, ref, p1_ss.at[o], p1_rs.at[o], partner)

    def p2_copy(o):
        return remote(tot, r2.at[o], p2_ss.at[o], p2_rs.at[o], dev((x + o) % NX, seg))

    def p3_copy(o):
        to = (seg + o) % SEG
        return remote(ret.at[to], r3.at[seg], p3_ss.at[o], p3_rs.at[o], dev(x, to))

    def p3_arrival(o):
        ref = r3.at[(seg - o + SEG) % SEG]
        return remote(ref, ref, p3_ss.at[o], p3_rs.at[o], partner)

    for o in FAR_FIRST:
        p1_copy(o).start()
    r1[seg] = state[seg]
    for piece in range(PIECES):
        project(wq, 0, piece)
    proj[0] = proj[0] * scale
    for o in range(1, SEG):
        p1_arrival(o).wait_recv()
    run = jnp.zeros((16, HEAD), F32)
    for i in range(SEG):
        run = run + r1[i].astype(F32)
    tot[...] = run
    for o in range(1, NX):
        @pl.when(x + o < NX)
        def _():
            p2_copy(o).start()

    row = lax.broadcasted_iota(jnp.int32, (TOK, TOK), 0)
    column = lax.broadcasted_iota(jnp.int32, (TOK, TOK), 1)
    for h in range(2):
        lanes = pl.ds(h * HEAD, HEAD)
        near = lax.dot_general(
            proj[0, :, lanes].astype(BF16), proj[1, :, lanes].astype(BF16), NT, preferred_element_type=F32
        )
        near = jnp.where(row >= column, near, 0.0).astype(BF16)
        mixed[:, lanes] = jnp.dot(near, proj[2, :, lanes].astype(BF16), preferred_element_type=F32)

    before[...] = jnp.zeros_like(before)
    for o in range(1, NX):
        @pl.when(x >= o)
        def _():
            p2_copy(o).wait_recv()
            before[...] += r2[o]
    run = before[...]
    for i in range(SEG):
        ret[i] = run.astype(BF16)
        run = run + r1[i].astype(F32)
    for o in FAR_FIRST:
        p3_copy(o).start()
    r3[seg] = ret[seg]
    for o in range(1, SEG):
        p3_arrival(o).wait_recv()

    for h in range(2):
        lanes = pl.ds(h * HEAD, HEAD)
        carried = r3[pl.ds(h * (SEG // 2), SEG // 2)].reshape(HEAD, HEAD)
        total = mixed[:, lanes] + jnp.dot(proj[0, :, lanes].astype(BF16), carried, preferred_element_type=F32)
        mean = jnp.mean(total * total, axis=1, keepdims=True)
        out[:, lanes] = (total * lax.rsqrt(mean + 1e-6)).astype(BF16)

    for which in (0, 1):
        for i in range(8):
            core_copy(i, 0, 0, which).wait_send()
        for i in range(7):
            kv_copy(i, which).wait_send()
    for o in range(1, NX):
        @pl.when(x >= o)
        def _():
            q_copy(o).wait_send()

        @pl.when(x + o < NX)
        def _():
            for copy in o_copies(o):
                copy.wait_send()
            p2_copy(o).wait_send()
    for direction in (0, 1):
        for piece in range(PIECES):
            for step in range(chain(direction, piece, 3)):
                rs_copy(direction, step, piece).wait_send()
            for distance in range(1, chain(direction, piece) + 1):
                ag_copy(direction, distance, piece).wait_send()
    weight_copy.wait_send()
    weight_share.wait_send()
    att_copy.wait_send()
    for o in range(1, SEG):
        p1_copy(o).wait_send()
        p3_copy(o).wait_send()


def body(*args):
    vmem = pl.BlockSpec(memory_space=pltpu.VMEM)
    anywhere = pl.BlockSpec(memory_space=pl.ANY)
    dma = pltpu.SemaphoreType.DMA
    scratch = [
        pltpu.VMEM((ROWS, D), BF16),
        pltpu.VMEM((4 * HEAD, D), BF16),
        pltpu.VMEM((D, 2 * HEAD), BF16),
        pltpu.VMEM((D, 2 * HEAD), BF16),
        pltpu.VMEM((D, 2 * HEAD), BF16),
        pltpu.VMEM((TOK, 2 * HEAD), BF16),
        pltpu.VMEM((NX, HEAD, QROWS), BF16),
        pltpu.VMEM((PAIRS, 2 * KROWS, HEAD), BF16),
        pltpu.VMEM((PAIRS, 2 * KROWS, HEAD), BF16),
        pltpu.VMEM((PAIRS, HEAD, 2 * KROWS), BF16),
        pltpu.VMEM((NX, HEAD, QROWS), F32),
        pltpu.VMEM((NX, 8, QROWS), F32),
        pltpu.VMEM((NX, HEAD, QROWS), BF16),
        pltpu.VMEM((NX, 8, QROWS), F32),
        pltpu.VMEM((NX, HEAD, QROWS), BF16),
        pltpu.VMEM((NX, 8, QROWS), F32),
        pltpu.VMEM((2, NPAIR, ROWS, 2 * HEAD), BF16),
        pltpu.VMEM((NPAIR, ROWS, D), F32),
        pltpu.VMEM((2, 3, PIECES, ROWS, WIDE), BF16),
        pltpu.VMEM((2, 3, PIECES, ROWS, WIDE), BF16),
        pltpu.VMEM((TOK, D), BF16),
        pltpu.VMEM((3, TOK, 2 * HEAD), F32),
        pltpu.VMEM((NPAIR, ROWS, 2 * HEAD), BF16),
        pltpu.VMEM((SEG, 16, HEAD), BF16),
        pltpu.VMEM((SEG, 16, HEAD), BF16),
        pltpu.VMEM((16, HEAD), F32),
        pltpu.VMEM((NX, 16, HEAD), F32),
        pltpu.VMEM((SEG, 16, HEAD), BF16),
        pltpu.VMEM((SEG, 16, HEAD), BF16),
        pltpu.VMEM((2 * HEAD, 2 * HEAD), F32),
        pltpu.VMEM((TOK, 2 * HEAD), F32),
        pltpu.VMEM((16, HEAD), F32),
        dma((8,)),
        dma((2,)),
        dma((2,)),
        dma((1,)),
        dma((1,)),
        dma((7, 2)),
        dma((7, 2)),
        dma((8, 2)),
        dma((8, 2)),
        dma((NX,)),
        dma((NX,)),
        dma((NX, 2)),
        dma((NX, 2)),
        dma((2, 3, PIECES)),
        dma((2, 3, PIECES)),
        dma((2, 6, PIECES)),
        dma((2, 6, PIECES)),
        dma((SEG,)),
        dma((SEG,)),
        dma((NX,)),
        dma((NX,)),
        dma((SEG,)),
        dma((SEG,)),
    ]
    return pl.pallas_call(
        kernel,
        out_shape=jax.ShapeDtypeStruct((TOK, 2 * HEAD), BF16),
        in_specs=[anywhere] * 8,
        out_specs=vmem,
        scratch_shapes=scratch,
        compiler_params=pltpu.CompilerParams(
            collective_id=0, has_side_effects=True, vmem_limit_bytes=60 * 1024 * 1024
        ),
    )(*args)


def solution(mesh):
    return jax.shard_map(
        body,
        mesh=mesh,
        in_specs=(
            P("ctx", None),
            P("ctx", "head"),
            P("ctx", "head"),
            P("ctx", "head"),
            P("head", None),
            P(None, "head"),
            P(None, "head"),
            P(None, "head"),
        ),
        out_specs=P("ctx", "head"),
        check_vma=False,
    )
```

```python
import math

import jax
import jax.numpy as jnp
from jax import lax
from jax.experimental import pallas as pl
from jax.experimental.pallas import tpu as pltpu
from jax.sharding import PartitionSpec as P

MESH = pl.DeviceIdType.MESH
HEAD = 128
TOK = 192
D = 4096
NX, NY, NZ = 4, 8, 12
SEG = 2 * NY
NPAIR = NZ // 2
ROWS = TOK // NZ
PIECES = 4
WIDE = D // PIECES
QROWS = 2 * TOK
KROWS = 2 * TOK
C2 = math.log2(math.e) / math.sqrt(HEAD)
F32, BF16 = jnp.float32, jnp.bfloat16
NT = (((1,), (1,)), ((), ()))
TN = (((0,), (0,)), ((), ()))
DIST = (1, -1, 2, -2, 3, -3, 4)
PAIRS = 4
PARENT = {1: 0, 2: 1, 3: 2, 4: 2, 5: 4, 6: 4}
FAR_FIRST = sorted(range(1, SEG), key=lambda o: -min(o, SEG - o))


def chain(direction, piece, far=6):
    return far if (direction == 0) == (piece < PIECES // 2) else far - 1


def kernel(
    hidden, query, key, value, w_out, w_q, w_k, w_v, out,
    hid, wo, wq, wk, wv,
    qin, qt, kb, vb, vt, acc, stat, ob, mlb, po, pml, att,
    branch, rs_send, rs_recv, normed, proj,
    att_in, state, r1, tot, r2, ret, r3, keypad, mixed, before,
    load_sem, w_ss, w_rs, a_ss, a_rs,
    kv_ss, kv_rs, core_ss, core_rs, q_ss, q_rs, o_ss, o_rs,
    rs_ss, rs_rs, ag_ss, ag_rs, p1_ss, p1_rs, p2_ss, p2_rs, p3_ss, p3_rs,
):
    c = lax.axis_index("ctx")
    z = lax.axis_index("head")
    x, seg = c // SEG, c % SEG
    y, core = seg // 2, seg % 2
    zpair, parity = z // 2, z % 2

    def dev(xx, ss):
        return {"ctx": xx * SEG + ss, "head": z}

    def zdev(step):
        return {"ctx": c, "head": (z + step + NZ) % NZ}

    def ydev(step):
        return dev(x, ((y + step + NY) % NY) * 2 + core)

    partner = dev(x, y * 2 + (1 - core))

    def remote(src, dst, send, recv, to):
        return pltpu.make_async_remote_copy(
            src_ref=src, dst_ref=dst, send_sem=send, recv_sem=recv, device_id=to, device_id_type=MESH
        )

    def half(buf, pair, place, mine=True):
        start = place * KROWS + (core if mine else 1 - core) * TOK
        return buf.at[pair, pl.ds(pl.multiple_of(start, TOK), TOK)]

    loads = [
        pltpu.make_async_copy(w_out, wo.at[pl.ds(0, 2 * HEAD)], load_sem.at[0]),
        pltpu.make_async_copy(hidden.at[pl.ds(pl.multiple_of(z * ROWS, ROWS), ROWS)], hid, load_sem.at[1]),
        pltpu.make_async_copy(w_k, wk, load_sem.at[2]),
        pltpu.make_async_copy(w_v, wv, load_sem.at[3]),
        pltpu.make_async_copy(w_q, wq, load_sem.at[4]),
    ]
    first_loads = [
        pltpu.make_async_copy(query, qin, load_sem.at[5]),
        pltpu.make_async_copy(key, half(kb, PAIRS - 1, 0), load_sem.at[6]),
        pltpu.make_async_copy(value, half(vb, PAIRS - 1, 0), load_sem.at[7]),
    ]
    for load in (*first_loads, loads[0]):
        load.start()

    barrier = pltpu.get_barrier_semaphore()
    for o in range(1, SEG):
        pl.semaphore_signal(barrier, inc=1, device_id=dev(x, (seg + o) % SEG), device_id_type=MESH)
    for o in range(1, NX):
        pl.semaphore_signal(barrier, inc=1, device_id=dev((x + o) % NX, seg), device_id_type=MESH)
    for o in (1, -1, 2, -2):
        pl.semaphore_signal(barrier, inc=1, device_id=zdev(o), device_id_type=MESH)

    for load in first_loads:
        load.wait()
    stacked = jnp.concatenate([qin[:, pl.ds(0, HEAD)], qin[:, pl.ds(HEAD, HEAD)]], axis=0)
    qt[0] = jnp.transpose(stacked.astype(F32)).astype(BF16)
    pl.semaphore_wait(barrier, SEG - 1 + NX - 1 + 4)

    def kv_copy(i, which):
        buf = (kb, vb)[which]
        if i < 4:
            source, step = half(buf, PAIRS - 1, 0), DIST[i]
        elif i < 6:
            source, step = half(buf, 1, i - 4), (1, -1)[i - 4]
        else:
            source, step = half(buf, 1, which), (2, -2)[which]
        target = half(buf, i // 2, i % 2 if i < 6 else 1)
        return remote(source, target, kv_ss.at[i, which], kv_rs.at[i, which], ydev(step))

    def kv_arrival(i, pair, place, which):
        ref = half((kb, vb)[which], pair, place)
        return remote(ref, ref, kv_ss.at[i, which], kv_rs.at[i, which], partner)

    def core_copy(i, pair, place, which):
        ref = half((kb, vb)[which], pair, place)
        return remote(ref, ref, core_ss.at[i, which], core_rs.at[i, which], partner)

    def core_arrival(i, pair, place, which):
        ref = half((kb, vb)[which], pair, place, False)
        return remote(ref, ref, core_ss.at[i, which], core_rs.at[i, which], partner)

    def q_copy(o):
        return remote(qt.at[0], qt.at[o], q_ss.at[o], q_rs.at[o], dev((x - o + NX) % NX, seg))

    def o_copies(o):
        to = dev((x + o) % NX, seg)
        return (
            remote(ob.at[o], po.at[o], o_ss.at[o, 0], o_rs.at[o, 0], to),
            remote(mlb.at[o], pml.at[o], o_ss.at[o, 1], o_rs.at[o, 1], to),
        )

    given = wo.at[pl.ds(pl.multiple_of(core * HEAD, HEAD), HEAD)]
    taken = wo.at[pl.ds(pl.multiple_of(2 * HEAD + core * HEAD, HEAD), HEAD)]
    twin = {"ctx": c, "head": zpair * 2 + 1 - parity}
    weight_copy = remote(given, taken, w_ss.at[0], w_rs.at[0], twin)
    weight_share = remote(taken, taken, w_ss.at[1], w_rs.at[1], partner)

    for i in (2, 3, 0, 1):
        for which in (0, 1):
            kv_copy(i, which).start()
    for which in (0, 1):
        core_copy(7, PAIRS - 1, 0, which).start()
    for o in range(1, NX):
        @pl.when(x >= o)
        def _():
            q_copy(o).start()
    loads[0].wait()
    weight_copy.start()
    for load in loads[1:]:
        load.start()

    def fold(o, scores, values):
        old_max = stat[o, pl.ds(0, 1), :]
        new_max = jnp.maximum(old_max, jnp.max(scores, axis=0, keepdims=True) * C2)
        weights = jnp.exp2(scores * C2 - new_max)
        factor = jnp.exp2(old_max - new_max)
        stat[o, pl.ds(0, 1), :] = new_max
        stat[o, pl.ds(1, 1), :] = stat[o, pl.ds(1, 1), :] * factor + jnp.sum(weights, axis=0, keepdims=True)
        acc[o] = acc[o] * factor + jnp.dot(values, weights.astype(BF16), preferred_element_type=F32)

    def turn_values(pair, place):
        rows = pl.ds(place * KROWS, KROWS)
        vt[pair, :, rows] = jnp.transpose(vb[pair, rows, :].astype(F32)).astype(BF16)

    acc[...] = jnp.zeros_like(acc)
    stat[...] = jnp.zeros_like(stat)
    stat[:, 0, :] = jnp.full((NX, QROWS), -1e30, F32)
    for which in (0, 1):
        core_arrival(7, PAIRS - 1, 0, which).wait_recv()
    turn_values(PAIRS - 1, 0)
    key_pos = lax.broadcasted_iota(jnp.int32, (KROWS, QROWS), 0)
    column = lax.broadcasted_iota(jnp.int32, (KROWS, QROWS), 1)
    query_pos = core * TOK + jnp.where(column >= TOK, column - TOK, column)
    own = jnp.dot(kb[PAIRS - 1, pl.ds(0, KROWS), :], qt[0], preferred_element_type=F32)
    fold(0, jnp.where(key_pos <= query_pos, own, -1e30), vt[PAIRS - 1, :, pl.ds(0, KROWS)])
    forwards = {(2, 0): ((6, 0), (4, 0)), (2, 1): ((4, 1),), (3, 0): ((5, 0),), (3, 1): ((6, 1), (5, 1))}

    def receive(i):
        pair, place = (i // 2, i % 2) if i < 6 else (PAIRS - 1, 1)
        for which in (0, 1):
            kv_arrival(i, pair, place, which).wait_recv()
            for j, w in forwards.get((i, which), ()):
                kv_copy(j, w).start()
            core_copy(i, pair, place, which).start()

    for i in (2, 3, 0, 1):
        receive(i)
    for o in range(1, NX):
        @pl.when(x + o < NX)
        def _():
            q_copy(o).wait_recv()

    def pair_step(pair, carry):
        @pl.when(pair == 2)
        def _():
            for i in (4, 5, 6):
                receive(i)

        @pl.when(pair < PAIRS - 1)
        def _():
            for place in (0, 1):
                for which in (0, 1):
                    core_arrival(2 * pair + place, pair, place, which).wait_recv()
            turn_values(pair, 0)

        @pl.when(pair == PAIRS - 1)
        def _():
            for which in (0, 1):
                core_arrival(6, PAIRS - 1, 1, which).wait_recv()

        turn_values(pair, 1)

        last = pair == PAIRS - 1
        away = pair + 1
        seen_0 = jnp.logical_and(jnp.logical_not(last), y >= away)
        seen_1 = jnp.where(last, y >= away, y + away >= NY)
        bias_0 = jnp.where(seen_0, 0.0, -1e30).astype(F32)
        bias_1 = jnp.where(seen_1, 0.0, -1e30).astype(F32)
        for count in range(NX):
            @pl.when(x == NX - 1 - count)
            def _():
                found = [jnp.dot(kb[pair], qt[o], preferred_element_type=F32) for o in range(count + 1)]
                found[0] = jnp.concatenate([found[0][:KROWS] + bias_0, found[0][KROWS:] + bias_1], axis=0)
                for o in range(count + 1):
                    fold(o, found[o], vt[pair])
        return carry

    lax.fori_loop(0, PAIRS, pair_step, 0)

    for o in range(1, NX):
        @pl.when(x + o < NX)
        def _():
            ob[o] = acc[o].astype(BF16)
            mlb[o] = stat[o]
            for copy in o_copies(o):
                copy.start()

    weight_copy.wait_recv()
    weight_share.start()

    for o in range(1, NX):
        @pl.when(x >= o)
        def _():
            for copy in o_copies(o):
                copy.wait_recv()
            old_max, part_max = stat[0, pl.ds(0, 1), :], pml[o, pl.ds(0, 1), :]
            new_max = jnp.maximum(old_max, part_max)
            factor = jnp.exp2(old_max - new_max)
            part_factor = jnp.exp2(part_max - new_max)
            stat[0, pl.ds(0, 1), :] = new_max
            stat[0, pl.ds(1, 1), :] = stat[0, pl.ds(1, 1), :] * factor + pml[o, pl.ds(1, 1), :] * part_factor
            acc[0] = acc[0] * factor + po[o].astype(F32) * part_factor

    attended = jnp.transpose(acc[0] / stat[0, pl.ds(1, 1), :])
    att_copy = remote(att.at[1 - parity], att_in, a_ss.at[0], a_rs.at[0], twin)
    for side in range(2):
        which = 1 - parity if side == 0 else parity
        for k in range(NPAIR):
            for h in range(2):
                even = attended[h * TOK + 2 * k * ROWS : h * TOK + (2 * k + 1) * ROWS]
                odd = attended[h * TOK + (2 * k + 1) * ROWS : h * TOK + (2 * k + 2) * ROWS]
                att[which, k, :, pl.ds(h * HEAD, HEAD)] = jnp.where(which == 0, even, odd).astype(BF16)
        if side == 0:
            att_copy.start()

    def project_out(rows, depth_start, piece):
        columns = pl.ds(piece * WIDE, WIDE)
        term = jnp.dot(
            rows.reshape(NPAIR * ROWS, 2 * HEAD), wo[pl.ds(depth_start, 2 * HEAD), columns], preferred_element_type=F32
        )
        return columns, term.reshape(NPAIR, ROWS, WIDE)

    for piece in range(PIECES):
        columns, term = project_out(att[parity], 0, piece)
        branch[:, :, columns] = term
    weight_share.wait_recv()
    att_copy.wait_recv()

    def rs_copy(direction, step, piece):
        return remote(
            rs_send.at[direction, step, piece],
            rs_recv.at[direction, step, piece],
            rs_ss.at[direction, step, piece],
            rs_rs.at[direction, step, piece],
            zdev(-2 if direction == 0 else 2),
        )

    for step in range(3):
        for piece in range(PIECES):
            if step == 0:
                columns, term = project_out(att_in[...], 2 * HEAD, piece)
                branch[:, :, columns] += term
            for direction in (0, 1):
                length = chain(direction, piece, 3)
                if step < length:
                    away = length - step
                    target = (zpair + (-away if direction == 0 else away) + NPAIR) % NPAIR
                    term = branch[target, :, pl.ds(piece * WIDE, WIDE)]
                    if step > 0:
                        rs_copy(direction, step - 1, piece).wait_recv()
                        term = term + rs_recv[direction, step - 1, piece].astype(F32)
                    rs_send[direction, step, piece] = term.astype(BF16)
                    rs_copy(direction, step, piece).start()

    def rows_of(direction, distance, piece):
        place = (z + (distance if direction == 0 else -distance) + NZ) % NZ
        rows = pl.ds(pl.multiple_of(place * ROWS, ROWS), ROWS)
        return normed.at[rows, pl.ds(piece * WIDE, WIDE)]

    def ag_remote(ref, direction, distance, piece, step):
        return remote(
            ref, ref, ag_ss.at[direction, distance - 1, piece], ag_rs.at[direction, distance - 1, piece],
            zdev(-step if direction == 0 else step),
        )

    def ag_copy(direction, distance, piece):
        parent = PARENT[distance]
        return ag_remote(rows_of(direction, parent, piece), direction, distance, piece, distance - parent)

    def ag_arrival(direction, distance, piece):
        return ag_remote(rows_of(direction, distance, piece), direction, distance, piece, 1)

    def pass_on(direction, distance, piece):
        for farther in (6, 5, 4, 3, 2, 1):
            if PARENT[farther] == distance and farther <= chain(direction, piece):
                ag_copy(direction, farther, piece).start()

    loads[1].wait()
    for piece in range(PIECES):
        columns = pl.ds(piece * WIDE, WIDE)
        total = branch[zpair, :, columns] + hid[:, columns].astype(F32)
        for direction in (0, 1):
            last = chain(direction, piece, 3) - 1
            rs_copy(direction, last, piece).wait_recv()
            total = total + rs_recv[direction, last, piece].astype(F32)
        normed[pl.ds(pl.multiple_of(z * ROWS, ROWS), ROWS), columns] = total.astype(BF16)
        for direction in (0, 1):
            pass_on(direction, 0, piece)

    def project(weight, slot, piece):
        columns = pl.ds(piece * WIDE, WIDE)
        proj[slot] += jnp.dot(normed[:, columns], weight[columns, :], preferred_element_type=F32)

    for load in loads[2:]:
        load.wait()
    proj[...] = jnp.zeros_like(proj)
    square = jnp.zeros((TOK, 1), F32)
    for distance in (1, 2, 4, 3, 6, 5):
        for piece in range(PIECES):
            for direction in (0, 1):
                if distance <= chain(direction, piece):
                    ag_arrival(direction, distance, piece).wait_recv()
                    pass_on(direction, distance, piece)
            if distance == 5:
                project(wk, 1, piece)
                project(wv, 2, piece)
                rows = normed[:, pl.ds(piece * WIDE, WIDE)].astype(F32)
                square = square + jnp.sum(rows * rows, axis=1, keepdims=True)
    scale = lax.rsqrt(square * (1.0 / D) + 1e-6)
    for slot in (1, 2):
        proj[slot] = proj[slot] * scale

    keypad[...] = jnp.zeros_like(keypad)
    keypad[pl.ds(0, TOK), :] = proj[1].astype(BF16).astype(F32)
    for h in range(2):
        lanes = pl.ds(h * HEAD, HEAD)
        turned = jnp.transpose(keypad[:, lanes])[:, :TOK].astype(BF16)
        part = jnp.dot(turned, proj[2, :, lanes].astype(BF16), preferred_element_type=F32)
        state[pl.ds(h * (SEG // 2), SEG // 2)] = part.astype(BF16).reshape(SEG // 2, 16, HEAD)

    def p1_copy(o):
        return remote(state.at[(seg + o) % SEG], r1.at[seg], p1_ss.at[o], p1_rs.at[o], dev(x, (seg + o) % SEG))

    def p1_arrival(o):
        ref = r1.at[(seg - o + SEG) % SEG]
        return remote(ref, ref, p1_ss.at[o], p1_rs.at[o], partner)

    def p2_copy(o):
        return remote(tot, r2.at[o], p2_ss.at[o], p2_rs.at[o], dev((x + o) % NX, seg))

    def p3_copy(o):
        to = (seg + o) % SEG
        return remote(ret.at[to], r3.at[seg], p3_ss.at[o], p3_rs.at[o], dev(x, to))

    def p3_arrival(o):
        ref = r3.at[(seg - o + SEG) % SEG]
        return remote(ref, ref, p3_ss.at[o], p3_rs.at[o], partner)

    for o in FAR_FIRST:
        p1_copy(o).start()
    r1[seg] = state[seg]
    for piece in range(PIECES):
        project(wq, 0, piece)
    proj[0] = proj[0] * scale
    for o in range(1, SEG):
        p1_arrival(o).wait_recv()
    run = jnp.zeros((16, HEAD), F32)
    for i in range(SEG):
        run = run + r1[i].astype(F32)
    tot[...] = run
    for o in range(1, NX):
        @pl.when(x + o < NX)
        def _():
            p2_copy(o).start()

    row = lax.broadcasted_iota(jnp.int32, (TOK, TOK), 0)
    column = lax.broadcasted_iota(jnp.int32, (TOK, TOK), 1)
    for h in range(2):
        lanes = pl.ds(h * HEAD, HEAD)
        near = lax.dot_general(
            proj[0, :, lanes].astype(BF16), proj[1, :, lanes].astype(BF16), NT, preferred_element_type=F32
        )
        near = jnp.where(row >= column, near, 0.0).astype(BF16)
        mixed[:, lanes] = jnp.dot(near, proj[2, :, lanes].astype(BF16), preferred_element_type=F32)

    before[...] = jnp.zeros_like(before)
    for o in range(1, NX):
        @pl.when(x >= o)
        def _():
            p2_copy(o).wait_recv()
            before[...] += r2[o]
    run = before[...]
    for i in range(SEG):
        ret[i] = run.astype(BF16)
        run = run + r1[i].astype(F32)
    for o in FAR_FIRST:
        p3_copy(o).start()
    r3[seg] = ret[seg]
    for o in range(1, SEG):
        p3_arrival(o).wait_recv()

    for h in range(2):
        lanes = pl.ds(h * HEAD, HEAD)
        carried = r3[pl.ds(h * (SEG // 2), SEG // 2)].reshape(HEAD, HEAD)
        total = mixed[:, lanes] + jnp.dot(proj[0, :, lanes].astype(BF16), carried, preferred_element_type=F32)
        mean = jnp.mean(total * total, axis=1, keepdims=True)
        out[:, lanes] = (total * lax.rsqrt(mean + 1e-6)).astype(BF16)

    for which in (0, 1):
        for i in range(8):
            core_copy(i, 0, 0, which).wait_send()
        for i in range(7):
            kv_copy(i, which).wait_send()
    for o in range(1, NX):
        @pl.when(x >= o)
        def _():
            q_copy(o).wait_send()

        @pl.when(x + o < NX)
        def _():
            for copy in o_copies(o):
                copy.wait_send()
            p2_copy(o).wait_send()
    for direction in (0, 1):
        for piece in range(PIECES):
            for step in range(chain(direction, piece, 3)):
                rs_copy(direction, step, piece).wait_send()
            for distance in range(1, chain(direction, piece) + 1):
                ag_copy(direction, distance, piece).wait_send()
    weight_copy.wait_send()
    weight_share.wait_send()
    att_copy.wait_send()
    for o in range(1, SEG):
        p1_copy(o).wait_send()
        p3_copy(o).wait_send()


def body(*args):
    vmem = pl.BlockSpec(memory_space=pltpu.VMEM)
    anywhere = pl.BlockSpec(memory_space=pl.ANY)
    dma = pltpu.SemaphoreType.DMA
    scratch = [
        pltpu.VMEM((ROWS, D), BF16),
        pltpu.VMEM((4 * HEAD, D), BF16),
        pltpu.VMEM((D, 2 * HEAD), BF16),
        pltpu.VMEM((D, 2 * HEAD), BF16),
        pltpu.VMEM((D, 2 * HEAD), BF16),
        pltpu.VMEM((TOK, 2 * HEAD), BF16),
        pltpu.VMEM((NX, HEAD, QROWS), BF16),
        pltpu.VMEM((PAIRS, 2 * KROWS, HEAD), BF16),
        pltpu.VMEM((PAIRS, 2 * KROWS, HEAD), BF16),
        pltpu.VMEM((PAIRS, HEAD, 2 * KROWS), BF16),
        pltpu.VMEM((NX, HEAD, QROWS), F32),
        pltpu.VMEM((NX, 8, QROWS), F32),
        pltpu.VMEM((NX, HEAD, QROWS), BF16),
        pltpu.VMEM((NX, 8, QROWS), F32),
        pltpu.VMEM((NX, HEAD, QROWS), BF16),
        pltpu.VMEM((NX, 8, QROWS), F32),
        pltpu.VMEM((2, NPAIR, ROWS, 2 * HEAD), BF16),
        pltpu.VMEM((NPAIR, ROWS, D), F32),
        pltpu.VMEM((2, 3, PIECES, ROWS, WIDE), BF16),
        pltpu.VMEM((2, 3, PIECES, ROWS, WIDE), BF16),
        pltpu.VMEM((TOK, D), BF16),
        pltpu.VMEM((3, TOK, 2 * HEAD), F32),
        pltpu.VMEM((NPAIR, ROWS, 2 * HEAD), BF16),
        pltpu.VMEM((SEG, 16, HEAD), BF16),
        pltpu.VMEM((SEG, 16, HEAD), BF16),
        pltpu.VMEM((16, HEAD), F32),
        pltpu.VMEM((NX, 16, HEAD), F32),
        pltpu.VMEM((SEG, 16, HEAD), BF16),
        pltpu.VMEM((SEG, 16, HEAD), BF16),
        pltpu.VMEM((2 * HEAD, 2 * HEAD), F32),
        pltpu.VMEM((TOK, 2 * HEAD), F32),
        pltpu.VMEM((16, HEAD), F32),
        dma((8,)),
        dma((2,)),
        dma((2,)),
        dma((1,)),
        dma((1,)),
        dma((7, 2)),
        dma((7, 2)),
        dma((8, 2)),
        dma((8, 2)),
        dma((NX,)),
        dma((NX,)),
        dma((NX, 2)),
        dma((NX, 2)),
        dma((2, 3, PIECES)),
        dma((2, 3, PIECES)),
        dma((2, 6, PIECES)),
        dma((2, 6, PIECES)),
        dma((SEG,)),
        dma((SEG,)),
        dma((NX,)),
        dma((NX,)),
        dma((SEG,)),
        dma((SEG,)),
    ]
    return pl.pallas_call(
        kernel,
        out_shape=jax.ShapeDtypeStruct((TOK, 2 * HEAD), BF16),
        in_specs=[anywhere] * 8,
        out_specs=vmem,
        scratch_shapes=scratch,
        compiler_params=pltpu.CompilerParams(
            collective_id=0, has_side_effects=True, vmem_limit_bytes=60 * 1024 * 1024
        ),
    )(*args)


def solution(mesh):
    return jax.shard_map(
        body,
        mesh=mesh,
        in_specs=(
            P("ctx", None),
            P("ctx", "head"),
            P("ctx", "head"),
            P("ctx", "head"),
            P("head", None),
            P(None, "head"),
            P(None, "head"),
            P(None, "head"),
        ),
        out_specs=P("ctx", "head"),
        check_vma=False,
    )
```
